128 devices in a mesh: wide: 32 (over z, y, core), narrow: 4 (over x).
Axes of the slice: x: 4, y: 4, z: 4, core: 2. Of those that a mesh axis runs over, the one named last changes fastest.
Arguments:
- embeddings: bfloat16 [384, 256, 768], P(('wide', 'narrow'))
- seeds: float32 [384, 256, 64], P(('wide', 'narrow')), may hold values from -6 to 6
- neighbours: int32 [384, 32], P(('wide', 'narrow')), may hold values from -1 to 383, as said below
Outputs:
- scores: float32 [384, 256, 64], P(('wide', 'narrow'))
The draws below stay inside these ranges and needn't reach their ends.
Inputs may be any that keep to these rules, and one draw needn't show every extreme that they name: `neighbours`: A block's used slots come first and name distinct blocks other than itself, each on a device whose wide index differs from the block's own by at most 2 around the cycle; between 16 and 32 slots of a block are used, all 32 in some block.
All inputs are finite; a program needn't handle non-finite values.
Results may differ from the reference program's by a relative error of at most 0.0013.
Values may be sent and summed in bfloat16 or wider, within the bound.
No kernel may reach another device: no remote copies, remote signals or barrier semaphores. Data moves between devices by JAX's collectives and lax.ppermute only.
A program may use at most 192 MiB of HBM per device.

```python
import math
import jax
import jax.numpy as jnp
from jax import lax

D = 768
CH = 64
ROWS = 256
NBR = 32
ITERS = 3
BLK_DEV = 3
N_WIDE = 32
N_NARROW = 4


def prototype_ids(key):
    blocks_all = BLK_DEV * N_WIDE * N_NARROW
    prototype_count = max(ROWS * NBR // 16, 8)
    return jax.random.randint(jax.random.fold_in(key, 101), (blocks_all, ROWS), 0, prototype_count)


def draw_embeddings(key, part):
    picked = prototype_ids(key)
    key = jax.random.fold_in(key, 3)
    blocks_all = BLK_DEV * N_WIDE * N_NARROW
    prototype_count = max(ROWS * NBR // 16, 8)
    key_centre, key_noise, key_scale = jax.random.split(key, 3)
    centres = jax.random.normal(key_centre, (prototype_count, D), jnp.float32)
    noise = 0.5 * jax.random.normal(key_noise, (blocks_all, ROWS, D), jnp.float32)
    base = centres[picked] + noise
    scale = jnp.exp(jax.random.uniform(key_scale, (blocks_all, ROWS, 1), jnp.float32, 0.0, math.log(10.0)))
    return (base * scale * 0.3).astype(jnp.bfloat16)


def draw_seeds(key, part):
    picked = prototype_ids(key)
    key = jax.random.fold_in(key, 5)
    blocks_all = BLK_DEV * N_WIDE * N_NARROW
    prototype_count = max(ROWS * NBR // 16, 8)
    key_label, key_noise = jax.random.split(key)
    labels = jax.random.normal(key_label, (prototype_count, CH), jnp.float32)
    noise = 0.7 * jax.random.normal(key_noise, (blocks_all, ROWS, CH), jnp.float32)
    return jnp.clip(labels[picked] + noise, -6.0, 6.0).astype(jnp.float32)


def draw_neighbours(key, part):
    total = BLK_DEV * N_WIDE * N_NARROW
    reach = 5 * N_NARROW * BLK_DEV
    key_order, key_count = jax.random.split(jax.random.fold_in(key, 7))
    blocks = jnp.arange(total, dtype=jnp.int32)
    cycle_pos = blocks // BLK_DEV // N_NARROW
    slots = jnp.arange(reach, dtype=jnp.int32)
    offset = slots // (N_NARROW * BLK_DEV) - 2
    within = slots % (N_NARROW * BLK_DEV)
    ids = (cycle_pos[:, None] + offset[None, :]) % N_WIDE * (N_NARROW * BLK_DEV) + within[None, :]
    ranks = jax.random.randint(key_order, (total, reach), 0, 1 << 20)
    ranks = jnp.where(ids == blocks[:, None], 1 << 21, ranks)
    order = jnp.argsort(ranks, axis=1, stable=True)[:, :NBR]
    chosen = jnp.take_along_axis(ids, order, axis=1)
    count = jax.random.randint(key_count, (total,), NBR // 2, NBR + 1)
    count = count.at[0].set(NBR)
    used = jnp.arange(NBR, dtype=jnp.int32)[None, :] < count[:, None]
    return jnp.where(used, chosen, -1).astype(jnp.int32)


def setup_inputs(seed: int = 0) -> dict:
    keys = jax.random.split(jax.random.key(seed), 4)
    return {
        "embeddings": draw_embeddings(jax.random.fold_in(keys[3], 71), 0),
        "seeds": draw_seeds(jax.random.fold_in(keys[3], 71), 0),
        "neighbours": draw_neighbours(jax.random.fold_in(keys[3], 71), 0),
    }


SHARP = 24.0
ALPHA = 0.8
EPS = 1e-06

def unit_rows(embeddings):
    values = embeddings.astype(jnp.float32)
    return (values * lax.rsqrt(lax.optimization_barrier(jnp.sum(values * values, axis=-1, keepdims=True)) + EPS)).astype(jnp.bfloat16)

def reference(embeddings, seeds, neighbours):
    units = unit_rows(embeddings)
    valid = neighbours >= 0
    ids = jnp.maximum(neighbours, 0).astype(jnp.int32)

    def one_block(items):
        own, node_ids, usable = items
        near_units = units[node_ids].astype(jnp.float32)
        cosine = jnp.einsum('rd,kqd->krq', own.astype(jnp.float32), near_units)
        weight = jnp.where(usable[:, None, None], jnp.exp(SHARP * cosine), 0.0)
        degree = lax.optimization_barrier(jnp.sum(weight, axis=(0, 2)))
        return (weight.astype(jnp.bfloat16), degree)
    wround, degree = lax.map(one_block, (units, ids, valid))
    state = seeds.astype(jnp.bfloat16)
    scores = seeds
    for step in range(ITERS):

        def spread_block(items):
            tiles, node_ids, block_degree = items
            near_state = state[node_ids].astype(jnp.float32)
            spread = jnp.einsum('krq,kqh->rh', tiles.astype(jnp.float32), near_state)
            return spread / block_degree[:, None]
        spread = lax.map(spread_block, (wround, ids, degree))
        scores = ALPHA * spread + (1.0 - ALPHA) * seeds
        state = scores.astype(jnp.bfloat16)
    return scores
```

```python
import functools
import math

import jax
import jax.numpy as jnp
from jax import lax
from jax.experimental import pallas as pl
from jax.experimental.pallas import tpu as pltpu
from jax.sharding import Mesh, PartitionSpec as P

NBR = 32
ITERS = 3
SHARP = 24.0
ALPHA = 0.8
EPS = 1e-06
ROWS = 256
D = 768
CH = 64
BLK = 3
NX = 4
NW = 32
HALF = BLK * ROWS // 2
SCALE = SHARP * math.log2(math.e)
WIDE = ("z", "y", "c")
VM = pl.BlockSpec(memory_space=pltpu.VMEM)
SM = pl.BlockSpec(memory_space=pltpu.SMEM)
F32 = jnp.float32
BF16 = jnp.bfloat16


def along_x(v, by):
    return lax.ppermute(v, "x", [(i, (i + by) % NX) for i in range(NX)])


def from_wide(v, offset):
    return lax.ppermute(v, WIDE, [((i + offset) % NW, i) for i in range(NW)])


def swap_core(v):
    return lax.ppermute(v, "c", [(0, 1), (1, 0)])


def prep_kernel(emb_ref, seed_ref, low_ref, high_ref, full_ref, state_ref):
    for block in range(BLK):
        values = emb_ref[block].astype(F32)
        total = jnp.sum(values * values, axis=-1, keepdims=True)
        unit = (values * lax.rsqrt(total + EPS)).astype(BF16)
        full_ref[block] = unit
        state_ref[block] = seed_ref[block].astype(BF16)
    low_ref[0:256] = full_ref[0]
    low_ref[256:384] = full_ref[1, 0:128]
    high_ref[0:128] = full_ref[1, 128:256]
    high_ref[128:384] = full_ref[2]


def prepare(embeddings, seeds_t):
    return pl.pallas_call(
        prep_kernel,
        out_shape=(
            jax.ShapeDtypeStruct((HALF, D), BF16),
            jax.ShapeDtypeStruct((HALF, D), BF16),
            jax.ShapeDtypeStruct((BLK, ROWS, D), BF16),
            jax.ShapeDtypeStruct((BLK, CH, ROWS), BF16),
        ),
        in_specs=[VM, VM],
        out_specs=(VM, VM, VM, VM),
        compiler_params=pltpu.CompilerParams(vmem_limit_bytes=16 << 20),
        cost_estimate=pl.CostEstimate(flops=2_000_000, bytes_accessed=5_000_000, transcendentals=768),
        name="prep",
    )(embeddings, seeds_t)


def build_kernel(n_rows, n_cols, has_acc, *refs):
    refs = list(refs)
    mask_ref = refs.pop(0)
    row_refs = [refs.pop(0) for _ in range(n_rows)]
    col_refs = [refs.pop(0) for _ in range(n_cols)]
    state_refs = [refs.pop(0) for _ in range(n_cols)]
    acc_in = [refs.pop(0) for _ in has_acc if _]
    deg_in = [refs.pop(0) for _ in has_acc if _]
    w_ref, acc_ref, deg_ref = refs
    at = 0
    for group in range(n_rows):
        here = pl.ds(group * BLK, BLK)
        if has_acc[group]:
            acc_ref[here] = acc_in[at][...]
            deg_ref[here] = deg_in[at][...]
            at += 1
        else:
            acc_ref[here] = jnp.zeros((BLK, CH, ROWS), F32)
            deg_ref[here] = jnp.zeros((BLK, 8, ROWS), F32)
    width = n_cols * BLK
    for group in range(n_rows):
        for source in range(n_cols):

            @pl.loop(0, BLK * BLK)
            def _(step):
                i = step // BLK
                j = step - i * BLK
                row = group * BLK + i
                slot = row * width + source * BLK + j

                @pl.when(mask_ref[slot] != 0)
                def _():
                    cosine = lax.dot_general(
                        col_refs[source][j],
                        row_refs[group][i],
                        (((1,), (1,)), ((), ())),
                        preferred_element_type=F32,
                    )
                    weight = jnp.exp2(cosine * SCALE)
                    deg_ref[row] += jnp.sum(weight.reshape(ROWS // 8, 8, ROWS), axis=0)
                    rounded = weight.astype(BF16)
                    w_ref[slot] = rounded
                    acc_ref[row] += jnp.dot(
                        state_refs[source][j], rounded, preferred_element_type=F32
                    )


def build(mask, rows, cols, states, accs, degs):
    n_rows, n_cols = len(rows), len(cols)
    has_acc = tuple(a is not None for a in accs)
    slots = n_rows * BLK * n_cols * BLK
    given = [a for a in accs if a is not None] + [d for d in degs if d is not None]
    operands = [mask, *rows, *cols, *states, *given]
    return pl.pallas_call(
        functools.partial(build_kernel, n_rows, n_cols, has_acc),
        out_shape=(
            jax.ShapeDtypeStruct((slots, ROWS, ROWS), BF16),
            jax.ShapeDtypeStruct((n_rows * BLK, CH, ROWS), F32),
            jax.ShapeDtypeStruct((n_rows * BLK, 8, ROWS), F32),
        ),
        in_specs=[SM] + [VM] * (len(operands) - 1),
        out_specs=(VM, VM, VM),
        compiler_params=pltpu.CompilerParams(vmem_limit_bytes=32 << 20),
        cost_estimate=pl.CostEstimate(
            flops=slots * 40_000_000, bytes_accessed=slots * 131072, transcendentals=slots * 26000
        ),
        name=f"build_{n_rows}_{n_cols}",
    )(*operands)


def spread_kernel(plan, n_w, mask_ref, *refs):
    w_refs = refs[:n_w]
    state_refs = refs[n_w:-1]
    acc_ref = refs[-1]

    @pl.loop(0, NX * BLK)
    def _(row):
        acc_ref[row] = jnp.zeros((CH, ROWS), F32)

    for group, pieces in enumerate(plan):
        for which, first_row, width, first_col, source in pieces:

            @pl.loop(0, BLK * BLK)
            def _(step):
                i = step // BLK
                j = step - i * BLK
                row = group * BLK + i

                @pl.when(mask_ref[row * 15 + source * BLK + j] != 0)
                def _():
                    slot = (first_row + i) * width + first_col + j
                    acc_ref[row] += jnp.dot(
                        state_refs[source][j], w_refs[which][slot], preferred_element_type=F32
                    )


def spread(plan, mask, weights, states):
    return pl.pallas_call(
        functools.partial(spread_kernel, plan, len(weights)),
        out_shape=jax.ShapeDtypeStruct((NX * BLK, CH, ROWS), F32),
        in_specs=[SM] + [VM] * (len(weights) + len(states)),
        out_specs=VM,
        compiler_params=pltpu.CompilerParams(vmem_limit_bytes=40 << 20),
        cost_estimate=pl.CostEstimate(flops=75 * 8_400_000, bytes_accessed=10_000_000, transcendentals=0),
        name="spread",
    )(mask, *weights, *states)


def wide_exchange(v, core):
    below = from_wide(v, -2)
    above = from_wide(v, 2)
    partner = swap_core(v)
    across = swap_core(jnp.where(core == 0, above, below))
    return [v, partner, below, above, across]


def local(embeddings, seeds, neighbours):
    core = lax.axis_index("c")
    here_x = lax.axis_index("x")
    here_w = lax.axis_index(WIDE)
    seeds_t = jnp.swapaxes(seeds, 1, 2)
    low, high, units, state = prepare(embeddings, seeds_t)

    left_low = along_x(low, 1)
    right_high = along_x(high, -1)
    below = from_wide(units, -2)
    above = from_wide(units, 2)
    left_high = along_x(high, 1)
    right_low = along_x(low, -1)
    partner = swap_core(units)
    far_low = along_x(left_low, 1)
    far_high = along_x(right_high, -1)
    across = swap_core(jnp.where(core == 0, above, below))
    join = lambda a, b: jnp.concatenate([a, b], 0).reshape(BLK, ROWS, D)
    left = join(left_low, left_high)
    right = join(right_low, right_high)
    far = join(far_low, far_high)

    lists = jnp.concatenate(
        [neighbours, along_x(neighbours, 1), along_x(neighbours, -1), along_x(neighbours, 2)], 0
    )
    wides = jnp.stack(
        [here_w, here_w + 1 - 2 * core, here_w - 2, here_w + 2, here_w - 1 + 2 * core]
    ) % NW
    ids = ((wides[:, None] * NX + here_x) * BLK + jnp.arange(BLK)[None, :]).reshape(-1)
    used = jnp.any(lists[:, :, None] == ids[None, None, :], axis=1).astype(jnp.int32)

    states = wide_exchange(state, core)
    w0, acc0, deg0 = build(
        used[:3, :6].reshape(-1), [units], [units, partner], states[:2], [None], [None]
    )
    w1, acc1, deg1 = build(
        used[3:9, :6].reshape(-1), [left, right], [units, partner], states[:2], [None] * 2, [None] * 2
    )
    w2, acc2, deg2 = build(
        used[:9, 6:].reshape(-1), [units, left, right], [below, above, across], states[2:],
        [acc0, acc1[:3], acc1[3:]], [deg0, deg1[:3], deg1[3:]],
    )
    w3, acc3, deg3 = build(
        used[9:].reshape(-1), [far], [units, partner, below, above, across], states, [None], [None]
    )
    weights = [w0, w1, w2, w3]
    plan = (
        [(0, 0, 6, 0, 0), (0, 0, 6, 3, 1), (2, 0, 9, 0, 2), (2, 0, 9, 3, 3), (2, 0, 9, 6, 4)],
        [(1, 0, 6, 0, 0), (1, 0, 6, 3, 1), (2, 3, 9, 0, 2), (2, 3, 9, 3, 3), (2, 3, 9, 6, 4)],
        [(1, 3, 6, 0, 0), (1, 3, 6, 3, 1), (2, 6, 9, 0, 2), (2, 6, 9, 3, 3), (2, 6, 9, 6, 4)],
        [(3, 0, 15, 0, 0), (3, 0, 15, 3, 1), (3, 0, 15, 6, 2), (3, 0, 15, 9, 3), (3, 0, 15, 12, 4)],
    )

    def reduce_rows(own, to_left, to_right, to_far):
        return own + along_x(to_far, 2) + along_x(to_left, -1) + along_x(to_right, 1)

    wide_acc = jnp.concatenate([acc2, deg2], 1)
    far_acc = jnp.concatenate([acc3, deg3], 1)
    total = reduce_rows(wide_acc[:3], wide_acc[3:6], wide_acc[6:], far_acc)
    degree = jnp.sum(total[:, CH:], axis=1, keepdims=True)
    scale = ALPHA / degree
    prior = (1.0 - ALPHA) * seeds_t
    scores = total[:, :CH] * scale + prior
    flat = used.reshape(-1)
    for _ in range(ITERS - 1):
        states = wide_exchange(scores.astype(BF16), core)
        acc = spread(plan, flat, weights, states)
        total = reduce_rows(acc[:3], acc[3:6], acc[6:9], acc[9:])
        scores = total * scale + prior
    return jnp.swapaxes(scores, 1, 2)


def solution(mesh):
    fine = Mesh(mesh.devices.reshape(4, 4, 2, 4), ("z", "y", "c", "x"))
    everywhere = ("z", "y", "c", "x")
    return jax.shard_map(
        local,
        mesh=fine,
        in_specs=(P(everywhere, None, None), P(everywhere, None, None), P(everywhere, None)),
        out_specs=P(everywhere, None, None),
        check_vma=False,
    )
```

```python
import functools
import math

import jax
import jax.numpy as jnp
from jax import lax
from jax.experimental import pallas as pl
from jax.experimental.pallas import tpu as pltpu
from jax.sharding import Mesh, PartitionSpec as P

NBR = 32
ITERS = 3
SHARP = 24.0
ALPHA = 0.8
EPS = 1e-06
ROWS = 256
D = 768
CH = 64
BLK = 3
NX = 4
NW = 32
SCALE = SHARP * math.log2(math.e)
WIDE = ("z", "y", "c")
VM = pl.BlockSpec(memory_space=pltpu.VMEM)
SM = pl.BlockSpec(memory_space=pltpu.SMEM)
F32 = jnp.float32
BF16 = jnp.bfloat16
FIRST = (0, 48, 96, 176)
CAPS = (36, 36, 64, 48)
CHUNK_ROWS = ((0, 1, 2, 3, 4, 8), (0, 1, 2, 3, 4, 8), (0, 1, 2, 3, 4, 8, 5, 6, 7), (9, 10, 11))
CHUNK_COLS = ((0, 6), (6, 12), (0, 15), (0, 15))
COUNTS = 240
LISTS = 256
SPARE = NX * BLK
SUMS = CH + 8
CHEAP = pl.CostEstimate(flops=1000, bytes_accessed=1000, transcendentals=0)


def along_x(v, sign):
    pairs = []
    for core in range(2):
        by = sign if core == 0 else -sign
        pairs += [(core * NX + x, core * NX + (x + by) % NX) for x in range(NX)]
    return lax.ppermute(v, ("c", "x"), pairs)


def across_x(v):
    return lax.ppermute(v, "x", [(x, (x + 2) % NX) for x in range(NX)])


def from_wide(v, sign):
    return lax.ppermute(
        v, WIDE, [((i + (2 * sign if i % 2 == 0 else -2 * sign)) % NW, i) for i in range(NW)]
    )


def swap_core(v):
    return lax.ppermute(v, "c", [(0, 1), (1, 0)])


def prep_kernel(emb_ref, seed_ref, two_ref, one_ref, full_ref):
    for block in range(BLK):
        values = emb_ref[block].astype(F32)
        total = jnp.sum(values * values, axis=-1, keepdims=True)
        unit = (values * lax.rsqrt(total + EPS)).astype(BF16)
        full_ref[block * ROWS : (block + 1) * ROWS] = unit
        full_ref[BLK * ROWS :, block * ROWS : (block + 1) * ROWS] = seed_ref[block].astype(BF16)
        if block < 2:
            two_ref[block * D : (block + 1) * D] = jnp.transpose(unit)
        else:
            one_ref[...] = jnp.transpose(unit)


def prepare(embeddings, seeds_t):
    return pl.pallas_call(
        prep_kernel,
        out_shape=(
            jax.ShapeDtypeStruct((2 * D, ROWS), BF16),
            jax.ShapeDtypeStruct((D, ROWS), BF16),
            jax.ShapeDtypeStruct((BLK * ROWS + CH, D), BF16),
        ),
        in_specs=[VM, VM],
        out_specs=(VM, VM, VM),
        compiler_params=pltpu.CompilerParams(vmem_limit_bytes=8 << 20),
        cost_estimate=CHEAP,
        name="prep",
    )(embeddings, seeds_t)


def plan_kernel(place_ref, own_ref, back_ref, fore_ref, far_ref, list_ref):
    wide, x = place_ref[0], place_ref[1]
    core = wide & 1
    partner = 3 - 2 * core
    first = 4 - 4 * core
    counts = [jnp.int32(0)] * 4
    for row in range(SPARE):
        ref = (own_ref, back_ref, fore_ref, far_ref)[row // BLK]
        chunks = [c for c in range(4) if row in CHUNK_ROWS[c]]
        code = (row * 16 + CHUNK_ROWS[chunks[0]].index(row)) * 16

        def body(k, carry, ref=ref, i=row % BLK, chunks=chunks, code=code):
            block = ref[i, k]
            device = (block * 43691) >> 17
            step = ((device >> 2) - wide + 2) & (NW - 1)
            source = jnp.where(
                step == 2,
                0,
                jnp.where(
                    step == partner,
                    1,
                    jnp.where(step == first, 2, jnp.where(step == 4 - first, 3, 4)),
                ),
            )
            column = source * BLK + block - BLK * device
            hit = jnp.where((block >= 0) & ((device & (NX - 1)) == x), 1, 0)
            if len(chunks) == 1:
                list_ref[FIRST[chunks[0]] + carry[0]] = code + column
                return (carry[0] + hit,)
            for c in chunks:
                list_ref[FIRST[c] + carry[c]] = code + column
            low = jnp.where(source < 2, hit, 0)
            high = jnp.where(source == 4, hit, 0)
            return (carry[0] + low, carry[1] + hit - low - high, carry[2] + high)

        got = lax.fori_loop(0, NBR, body, tuple(counts[c] for c in chunks))
        for c, n in zip(chunks, got):
            counts[c] = n
    for c in range(4):
        for pad in range(4):
            list_ref[FIRST[c] + counts[c] + pad] = SPARE * 256 + CHUNK_COLS[c][0]
        list_ref[COUNTS + c] = (counts[c] + 3) >> 2


def make_plan(place, own, back, fore, far):
    return pl.pallas_call(
        plan_kernel,
        out_shape=jax.ShapeDtypeStruct((LISTS,), jnp.int32),
        in_specs=[SM] * 5,
        out_specs=SM,
        cost_estimate=CHEAP,
        name="plan",
    )(place, own, back, fore, far)


def build_kernel(chunk, n_rows, n_cols, has_sums, *refs):
    refs = list(refs)
    list_ref = refs.pop(0)
    rows = [refs.pop(0) for _ in range(n_rows)]
    cols = [refs.pop(0) for _ in range(n_cols)]
    given = refs.pop(0) if has_sums else None
    w_ref = refs.pop(0)
    row_buf, col_buf, state_buf, sum_buf = refs[-4:]
    outs = refs[:-4]
    at = 0
    for ref in rows:
        row_buf[at : at + ref.shape[0]] = ref[...]
        at += ref.shape[0]
    for at, ref in enumerate(cols):
        col_buf[at * BLK * ROWS : (at + 1) * BLK * ROWS] = ref[: BLK * ROWS]
        for j in range(BLK):
            state_buf[at * BLK + j] = ref[BLK * ROWS :, j * ROWS : (j + 1) * ROWS]
    if has_sums:
        sum_buf[: given.shape[0]] = given[...]
    else:
        sum_buf[...] = jnp.zeros_like(sum_buf)
    base = CHUNK_COLS[chunk][0]
    steps = list_ref[COUNTS + chunk]

    def four_tiles(step, _):
        for k in range(4):
            n = 4 * step + k
            named = list_ref[FIRST[chunk] + n]
            col = (named & 15) - base
            cosine = jnp.dot(
                col_buf[pl.ds(pl.multiple_of(col * ROWS, ROWS), ROWS), :],
                row_buf[pl.ds(pl.multiple_of(((named >> 4) & 15) * D, D), D), :],
                preferred_element_type=F32,
            )
            weight = jnp.exp2(cosine * SCALE)
            w_ref[n] = weight.astype(BF16)
            sum_buf[named >> 8, CH:] += jnp.sum(weight.reshape(ROWS // 8, 8, ROWS), axis=0)
        return 0

    def four_spreads(step, _):
        for k in range(4):
            n = 4 * step + k
            named = list_ref[FIRST[chunk] + n]
            sum_buf[named >> 8, :CH] += jnp.dot(
                state_buf[(named & 15) - base], w_ref[n], preferred_element_type=F32
            )
        return 0

    lax.fori_loop(0, steps, four_tiles, 0)
    lax.fori_loop(0, steps, four_spreads, 0)
    at = BLK * (NX - 1) if chunk == 3 else 0
    for ref in outs:
        ref[...] = sum_buf[at : at + ref.shape[0]]
        at += ref.shape[0]


def build(chunk, lists, rows, cols, sums, out_rows):
    n_cols = len(cols)
    operands = [lists, *rows, *cols] + ([sums] if sums is not None else [])
    return pl.pallas_call(
        functools.partial(build_kernel, chunk, len(rows), n_cols, sums is not None),
        out_shape=(
            jax.ShapeDtypeStruct((CAPS[chunk], ROWS, ROWS), BF16),
            *[jax.ShapeDtypeStruct((n, SUMS, ROWS), F32) for n in out_rows],
        ),
        in_specs=[SM] + [VM] * (len(operands) - 1),
        out_specs=(VM,) * (len(out_rows) + 1),
        scratch_shapes=[
            pltpu.VMEM((sum(r.shape[0] for r in rows), ROWS), BF16),
            pltpu.VMEM((n_cols * BLK * ROWS, D), BF16),
            pltpu.VMEM((n_cols * BLK, CH, ROWS), BF16),
            pltpu.VMEM((SPARE + 1, SUMS, ROWS), F32),
        ],
        compiler_params=pltpu.CompilerParams(vmem_limit_bytes=(20 if chunk == 2 else 14) << 20),
        cost_estimate=CHEAP,
        name=f"build_{chunk}",
    )(*operands)


def spread_kernel(list_ref, *refs):
    w_refs, state_refs, outs, (sum_buf, state_buf) = refs[:4], refs[4:9], refs[9:13], refs[13:]
    sum_buf[...] = jnp.zeros_like(sum_buf)
    for at, ref in enumerate(state_refs):
        state_buf[at * BLK : (at + 1) * BLK] = ref[...]
    for chunk, w_ref in enumerate(w_refs):

        def four(step, _, chunk=chunk, w_ref=w_ref):
            for k in range(4):
                n = 4 * step + k
                named = list_ref[FIRST[chunk] + n]
                sum_buf[named >> 8] += jnp.dot(
                    state_buf[named & 15], w_ref[n], preferred_element_type=F32
                )
            return 0

        lax.fori_loop(0, list_ref[COUNTS + chunk], four, 0)
    for at, ref in enumerate(outs):
        ref[...] = sum_buf[at * BLK : (at + 1) * BLK]


def spread(lists, weights, states):
    return pl.pallas_call(
        spread_kernel,
        out_shape=(jax.ShapeDtypeStruct((BLK, CH, ROWS), F32),) * NX,
        in_specs=[SM] + [VM] * (len(weights) + len(states)),
        out_specs=(VM,) * NX,
        scratch_shapes=[
            pltpu.VMEM((SPARE + 1, CH, ROWS), F32),
            pltpu.VMEM((5 * BLK, CH, ROWS), BF16),
        ],
        compiler_params=pltpu.CompilerParams(vmem_limit_bytes=4 << 20),
        cost_estimate=CHEAP,
        name="spread",
    )(lists, *weights, *states)


def wide_exchange(v):
    one = from_wide(v, 1)
    partner = swap_core(v)
    other = from_wide(v, -1)
    across = swap_core(one)
    return [v, partner, one, other, across]


def reduce_rows(own, back, fore, far):
    return own + along_x(back, -1) + along_x(fore, 1) + across_x(far)


def local(embeddings, seeds, neighbours):
    place = jnp.stack([lax.axis_index(WIDE), lax.axis_index("x")]).astype(jnp.int32)
    seeds_t = jnp.swapaxes(seeds, 1, 2)
    listed = [along_x(neighbours, 1), along_x(neighbours, -1), across_x(neighbours)]
    two, one, full = prepare(embeddings, seeds_t)
    two, one, full, *listed = lax.optimization_barrier((two, one, full, *listed))
    after = lambda v, *done: lax.optimization_barrier((v, *done))[0]
    partner = swap_core(full)
    back_two = along_x(two, 1)
    fore_one = along_x(one, -1)
    above = from_wide(full, 1)
    below = from_wide(after(full, partner), -1)
    lists = make_plan(place, neighbours, *listed)
    far_two = along_x(after(back_two, lists), 1)
    far_one = along_x(after(fore_one, lists), -1)
    fore_two = along_x(after(two, fore_one, lists), -1)
    back_one = along_x(after(one, back_two, lists), 1)

    near = [two, one, back_two, fore_one]
    w0, sums = build(0, lists, near, [full, partner], None, (9,))
    beside = swap_core(after(above, back_one))
    cols = [full, partner, above, below, beside]
    w1, sums = build(1, lists, near, [above, below], sums, (9,))
    w2, own, back, fore = build(2, lists, [*near, back_one, fore_two], cols, sums, (BLK, BLK, BLK))
    w3, far = build(3, after(lists, own), [far_two, far_one], cols, None, (BLK,))
    weights = [w0, w1, w2, w3]

    total = reduce_rows(own, back, fore, far)
    scale = ALPHA / jnp.sum(total[:, CH:], axis=1, keepdims=True)
    prior = (1.0 - ALPHA) * seeds_t
    scores = total[:, :CH] * scale + prior
    for _ in range(ITERS - 1):
        states = wide_exchange(scores.astype(BF16))
        total = reduce_rows(*spread(lists, weights, states))
        scores = total * scale + prior
    return jnp.swapaxes(scores, 1, 2)


def solution(mesh):
    fine = Mesh(mesh.devices.reshape(4, 4, 2, 4), ("z", "y", "c", "x"))
    everywhere = ("z", "y", "c", "x")
    return jax.shard_map(
        local,
        mesh=fine,
        in_specs=(P(everywhere, None, None), P(everywhere, None, None), P(everywhere, None)),
        out_specs=P(everywhere, None, None),
        check_vma=False,
    )
```

```python
import functools
import math

import jax
import jax.numpy as jnp
from jax import lax
from jax.experimental import pallas as pl
from jax.experimental.pallas import tpu as pltpu
from jax.sharding import Mesh, PartitionSpec as P

NBR = 32
ITERS = 3
SHARP = 24.0
ALPHA = 0.8
EPS = 1e-06
ROWS = 256
D = 768
CH = 64
BLK = 3
NX = 4
NW = 32
SCALE = SHARP * math.log2(math.e)
WIDE = ("z", "y", "c")
VM = pl.BlockSpec(memory_space=pltpu.VMEM)
SM = pl.BlockSpec(memory_space=pltpu.SMEM)
F32 = jnp.float32
BF16 = jnp.bfloat16
FIRST = (0, 48, 96, 144, 192)
CAP = 36
BASE = (0, 6, 0, 6, 12)
CHUNKS = 5
SOON = (0, 1, 2, 3, 4, 8)
COUNTS = 240
TOTALS = 248
LISTS = 256
SPARE = NX * BLK
SUMS = CH + 8
IDS = 16
CHEAP = pl.CostEstimate(flops=1000, bytes_accessed=1000, transcendentals=0)
LONG = pl.CostEstimate(flops=30_000_000_000, bytes_accessed=1000, transcendentals=0)


def along_x(v, sign):
    pairs = []
    for core in range(2):
        by = sign if core == 0 else -sign
        pairs += [(core * NX + x, core * NX + (x + by) % NX) for x in range(NX)]
    return lax.ppermute(v, ("c", "x"), pairs)


def across_x(v):
    return lax.ppermute(v, "x", [(x, (x + 2) % NX) for x in range(NX)])


def from_wide(v, sign):
    return lax.ppermute(
        v, WIDE, [((i + (2 * sign if i % 2 == 0 else -2 * sign)) % NW, i) for i in range(NW)]
    )


def swap_core(v):
    return lax.ppermute(v, "c", [(0, 1), (1, 0)])


def prep_kernel(emb_ref, seed_ref, ids_ref, two_ref, one_ref, full_ref):
    for block in range(BLK):
        values = emb_ref[block].astype(F32)
        total = jnp.sum(values * values, axis=-1, keepdims=True)
        unit = (values * lax.rsqrt(total + EPS)).astype(BF16)
        full_ref[block * ROWS : (block + 1) * ROWS] = unit
        full_ref[BLK * ROWS :, block * ROWS : (block + 1) * ROWS] = seed_ref[block].astype(BF16)
        if block < 2:
            two_ref[block * D : (block + 1) * D] = jnp.transpose(unit)
        else:
            one_ref[:D] = jnp.transpose(unit)
    two_ref[2 * D :] = ids_ref[...]
    one_ref[D:] = ids_ref[...]


def prepare(embeddings, seeds_t, ids):
    return pl.pallas_call(
        prep_kernel,
        out_shape=(
            jax.ShapeDtypeStruct((2 * D + IDS, ROWS), BF16),
            jax.ShapeDtypeStruct((D + IDS, ROWS), BF16),
            jax.ShapeDtypeStruct((BLK * ROWS + CH, D), BF16),
        ),
        in_specs=[VM, VM, VM],
        out_specs=(VM, VM, VM),
        compiler_params=pltpu.CompilerParams(vmem_limit_bytes=8 << 20),
        cost_estimate=CHEAP,
        name="prep",
    )(embeddings, seeds_t, ids)


def split_ids(neighbours):
    shown = neighbours + 1
    parts = jnp.concatenate([shown >> 4, shown & 15], axis=1).astype(BF16)
    return jnp.pad(parts, ((0, IDS - BLK), (0, ROWS - 2 * NBR)))


def joined_ids(rows):
    parts = rows[-IDS:][:BLK].astype(jnp.int32)
    return parts[:, :NBR] * 16 + parts[:, NBR : 2 * NBR] - 1


def plan_kernel(groups, place_ref, *refs):
    id_refs = refs[: len(groups)]
    old_ref, list_ref = (refs[-2], refs[-1]) if len(refs) > len(groups) + 1 else (None, refs[-1])
    wide, x = place_ref[0], place_ref[1]
    core = wide & 1
    partner = 3 - 2 * core
    first = 4 - 4 * core
    if old_ref is None:
        counts = [jnp.int32(0)] * CHUNKS
    else:

        def copy(k, _):
            list_ref[k] = old_ref[k]
            return 0

        counts = [old_ref[TOTALS + c] for c in range(CHUNKS)]
        for c in range(2, CHUNKS):
            lax.fori_loop(FIRST[c], FIRST[c] + counts[c], copy, 0)
    for ref, group in zip(id_refs, groups):
        for i in range(BLK):
            row = group * BLK + i
            chunks = (0, 1, 4) if row in SOON else (2, 3, 4)

            def body(k, carry, ref=ref, i=i, row=row, chunks=chunks):
                block = ref[i, k]
                device = (block * 43691) >> 17
                step = ((device >> 2) - wide + 2) & (NW - 1)
                source = jnp.where(
                    step == 2,
                    0,
                    jnp.where(
                        step == partner,
                        1,
                        jnp.where(step == first, 2, jnp.where(step == 4 - first, 3, 4)),
                    ),
                )
                code = row * 16 + source * BLK + block - BLK * device
                hit = jnp.where((block >= 0) & ((device & (NX - 1)) == x), 1, 0)
                for c, n in zip(chunks, carry):
                    list_ref[FIRST[c] + n] = code
                low = jnp.where(source < 2, hit, 0)
                high = jnp.where(source == 4, hit, 0)
                return (carry[0] + low, carry[1] + hit - low - high, carry[2] + high)

            got = lax.fori_loop(0, NBR, body, tuple(counts[c] for c in chunks), unroll=4)
            for c, n in zip(chunks, got):
                counts[c] = n
    for c in range(CHUNKS):
        for pad in range(4):
            list_ref[FIRST[c] + counts[c] + pad] = SPARE * 16 + BASE[c]
        list_ref[COUNTS + c] = (counts[c] + 3) >> 2
        list_ref[TOTALS + c] = counts[c]


def make_plan(groups, place, ids, old=None):
    operands = [place, *ids] + ([old] if old is not None else [])
    return pl.pallas_call(
        functools.partial(plan_kernel, groups),
        out_shape=jax.ShapeDtypeStruct((LISTS,), jnp.int32),
        in_specs=[SM] * len(operands),
        out_specs=SM,
        compiler_params=pltpu.CompilerParams(vmem_limit_bytes=1 << 20),
        cost_estimate=LONG,
        name="plan",
    )(*operands)


def tiles(chunk, list_ref, row_ref, col_ref, state_ref, w_ref, sum_ref, base=0):
    steps = list_ref[COUNTS + chunk]

    def four_tiles(step, _):
        for k in range(4):
            n = 4 * step + k
            named = list_ref[FIRST[chunk] + n]
            row, col = named >> 4, (named & 15) - base
            place = jnp.where(row == SPARE, 0, row) * D
            cosine = jnp.dot(
                col_ref[pl.ds(pl.multiple_of(col * ROWS, ROWS), ROWS), :],
                row_ref[pl.ds(pl.multiple_of(place, D), D), :],
                preferred_element_type=F32,
            )
            weight = jnp.exp2(cosine * SCALE)
            w_ref[n] = weight.astype(BF16)
            sum_ref[row, CH:] += jnp.sum(weight.reshape(ROWS // 8, 8, ROWS), axis=0)
        return 0

    def four_spreads(step, _):
        for k in range(4):
            n = 4 * step + k
            named = list_ref[FIRST[chunk] + n]
            sum_ref[named >> 4, :CH] += jnp.dot(
                state_ref[(named & 15) - base], w_ref[n], preferred_element_type=F32
            )
        return 0

    lax.fori_loop(0, steps, four_tiles, 0)
    lax.fori_loop(0, steps, four_spreads, 0)


def put_rows(buf, refs, places):
    for ref, (at, n) in zip(refs, places):
        buf[at * D : (at + n) * D] = ref[: n * D]


def put_cols(buf, states, refs):
    for at, ref in enumerate(refs):
        buf[at * BLK * ROWS : (at + 1) * BLK * ROWS] = ref[: BLK * ROWS]
        for j in range(BLK):
            states[at * BLK + j] = ref[BLK * ROWS :, j * ROWS : (j + 1) * ROWS]


def build_0(list_ref, r0, r1, r2, r3, c0, c1, w_ref, sum_ref, rows, cols, states):
    put_rows(rows, (r0, r1, r2, r3), ((0, 2), (2, 1), (3, 2), (8, 1)))
    put_cols(cols, states, (c0, c1))
    sum_ref[...] = jnp.zeros_like(sum_ref)
    tiles(0, list_ref, rows, cols, states, w_ref, sum_ref)


def build_1(list_ref, rows, c0, c1, c2, c3, given, w_ref, sum_ref, cols, states):
    put_cols(cols, states, (c0, c1, c2, c3))
    sum_ref[...] = given[...]
    tiles(1, list_ref, rows, cols, states, w_ref, sum_ref)


def build_2(list_ref, old_rows, r0, r1, r2, r3, cols, states, given, w2_ref, w3_ref, sum_ref, rows):
    rows[: 5 * D] = old_rows[: 5 * D]
    rows[8 * D : 9 * D] = old_rows[8 * D :]
    put_rows(rows, (r0, r1, r2, r3), ((5, 1), (6, 2), (9, 2), (11, 1)))
    sum_ref[...] = given[...]
    tiles(2, list_ref, rows, cols, states, w2_ref, sum_ref)
    tiles(3, list_ref, rows, cols, states, w3_ref, sum_ref)


def build_3(list_ref, rows, c4, given, w_ref, *refs):
    outs, (sums, states) = refs[:NX], refs[NX:]
    sums[...] = given[...]
    for j in range(BLK):
        states[j] = c4[BLK * ROWS :, j * ROWS : (j + 1) * ROWS]
    tiles(4, list_ref, rows, c4, states, w_ref, sums, base=BASE[4])
    for at, ref in enumerate(outs):
        ref[...] = sums[at * BLK : (at + 1) * BLK]


def build(kernel, room, outs, scratch, *operands):
    return pl.pallas_call(
        kernel,
        out_shape=[jax.ShapeDtypeStruct(*o) for o in outs],
        in_specs=[SM if o.dtype == jnp.int32 else VM for o in operands],
        out_specs=[VM] * len(outs),
        scratch_shapes=[pltpu.VMEM(*s) for s in scratch],
        compiler_params=pltpu.CompilerParams(vmem_limit_bytes=room << 20),
        cost_estimate=LONG,
        name=kernel.__name__,
    )(*operands)


WEIGHTS = ((CAP, ROWS, ROWS), BF16)


def rows_of(n):
    return ((n * D, ROWS), BF16)


def columns(n):
    return [((n * BLK * ROWS, D), BF16), ((n * BLK, CH, ROWS), BF16)]


SUM_BUF = ((SPARE + 1, SUMS, ROWS), F32)


def add_spread(chunk, list_ref, w_ref, state_ref, sum_ref):
    def four(step, _):
        for k in range(4):
            n = 4 * step + k
            named = list_ref[FIRST[chunk] + n]
            sum_ref[named >> 4] += jnp.dot(
                state_ref[named & 15], w_ref[n], preferred_element_type=F32
            )
        return 0

    lax.fori_loop(0, list_ref[COUNTS + chunk], four, 0)


def spread_near(near_ref, list_ref, w0, w2, s0, s1, sum_ref, states):
    sum_ref[...] = jnp.zeros_like(sum_ref)
    for at, ref in enumerate((s0, s1)):
        states[at * BLK : (at + 1) * BLK] = ref[...]
    add_spread(0, near_ref, w0, states, sum_ref)
    add_spread(2, list_ref, w2, states, sum_ref)


def spread_rest(near_ref, list_ref, w1, w3, w4, s2, s3, s4, given, own, back, fore, far, sums, states):
    sums[...] = given[...]
    for at, ref in enumerate((s2, s3, s4)):
        states[(at + 2) * BLK : (at + 3) * BLK] = ref[...]
    add_spread(1, near_ref, w1, states, sums)
    add_spread(3, list_ref, w3, states, sums)
    add_spread(4, list_ref, w4, states, sums)
    for at, ref in enumerate((own, back, fore, far)):
        ref[...] = sums[at * BLK : (at + 1) * BLK]


def spread(lists, weights, states):
    sums = ((SPARE + 1, CH, ROWS), F32)
    held = ((5 * BLK, CH, ROWS), BF16)
    w0, w1, w2, w3, w4 = weights
    (near,) = build(spread_near, 3, [sums], [held], *lists, w0, w2, *states[:2])
    return build(
        spread_rest, 4, [((BLK, CH, ROWS), F32)] * NX, [sums, held], *lists, w1, w3, w4, *states[2:], near
    )


def wide_exchange(v):
    one = from_wide(v, 1)
    partner = swap_core(v)
    other = from_wide(v, -1)
    across = swap_core(one)
    return [v, partner, one, other, across]


def reduce_rows(own, back, fore, far):
    return own + along_x(back, -1) + along_x(fore, 1) + across_x(far)


def local(embeddings, seeds, neighbours):
    place = jnp.stack([lax.axis_index(WIDE), lax.axis_index("x")]).astype(jnp.int32)
    seeds_t = jnp.swapaxes(seeds, 1, 2)
    after = lambda v, *done: lax.optimization_barrier((v, *done))[0]
    two, one, full = prepare(embeddings, seeds_t, split_ids(neighbours))
    back_two = along_x(two, 1)
    fore_one = along_x(one, -1)
    above = from_wide(full, 1)
    below = from_wide(full, -1)
    back_one = along_x(one, 1)
    back_two, fore_one, back_one, late_full, late_two = lax.optimization_barrier(
        (back_two, fore_one, back_one, full, two)
    )
    partner = swap_core(late_full)
    far_two = along_x(back_two, 1)
    fore_two = along_x(late_two, -1)
    far_one = along_x(after(fore_one, partner), -1)

    near = make_plan((0, 1, 2), place, [neighbours, joined_ids(back_two), joined_ids(fore_one)])
    w0, sums, rows = build(
        build_0, 6, [WEIGHTS, SUM_BUF, rows_of(9)], columns(2),
        near, two, one, back_two, fore_one, full, partner,
    )
    beside = swap_core(after(above, sums))
    w1, sums, cols, states = build(
        build_1, 4, [WEIGHTS, SUM_BUF, *columns(4)], [], near, rows, full, partner, above, below, sums
    )
    lists = make_plan((3,), place, [joined_ids(after(far_two, sums))], near)
    w2, w3, sums, rows = build(
        build_2, 4, [WEIGHTS, WEIGHTS, SUM_BUF, rows_of(12)], [],
        lists, rows, back_one, fore_two, far_two, far_one, cols, states, sums,
    )
    w4, own, back, fore, far = build(
        build_3, 4, [WEIGHTS] + [((BLK, SUMS, ROWS), F32)] * NX, [SUM_BUF, ((BLK, CH, ROWS), BF16)],
        lists, rows, beside, sums,
    )
    lists = [near, lists]
    weights = [w0, w1, w2, w3, w4]

    total = reduce_rows(own, back, fore, far)
    scale = ALPHA / jnp.sum(total[:, CH:], axis=1, keepdims=True)
    prior = (1.0 - ALPHA) * seeds_t
    scores = total[:, :CH] * scale + prior
    for _ in range(ITERS - 1):
        states = wide_exchange(scores.astype(BF16))
        total = reduce_rows(*spread(lists, weights, states))
        scores = total * scale + prior
    return jnp.swapaxes(scores, 1, 2)


def solution(mesh):
    fine = Mesh(mesh.devices.reshape(4, 4, 2, 4), ("z", "y", "c", "x"))
    everywhere = ("z", "y", "c", "x")
    return jax.shard_map(
        local,
        mesh=fine,
        in_specs=(P(everywhere, None, None), P(everywhere, None, None), P(everywhere, None)),
        out_specs=P(everywhere, None, None),
        check_vma=False,
    )
```

```python
import functools
import math

import jax
import jax.numpy as jnp
from jax import lax
from jax.experimental import pallas as pl
from jax.experimental.pallas import tpu as pltpu
from jax.sharding import Mesh, PartitionSpec as P

NBR = 32
ITERS = 3
SHARP = 24.0
ALPHA = 0.8
EPS = 1e-06
ROWS = 256
D = 768
CH = 64
BLK = 3
NX = 4
NW = 32
SCALE = SHARP * math.log2(math.e)
WIDE = ("z", "y", "c")
VM = pl.BlockSpec(memory_space=pltpu.VMEM)
SM = pl.BlockSpec(memory_space=pltpu.SMEM)
F32 = jnp.float32
BF16 = jnp.bfloat16
FIRST = (0, 48, 96, 144, 192)
CAP = 40
BASE = (0, 6, 0, 6, 12)
CHUNKS = 5
SOON = (0, 1, 2, 3, 4, 8)
COUNTS = 240
TOTALS = 245
BEFORE = 250
LISTS = 256
STEP = 9
SPARE = NX * BLK
SUMS = CH + 8
IDS = 16
CHEAP = pl.CostEstimate(flops=1000, bytes_accessed=1000, transcendentals=0)
LONG = pl.CostEstimate(flops=30_000_000_000, bytes_accessed=1000, transcendentals=0)


def along_x(v, sign):
    pairs = []
    for core in range(2):
        by = sign if core == 0 else -sign
        pairs += [(core * NX + x, core * NX + (x + by) % NX) for x in range(NX)]
    return lax.ppermute(v, ("c", "x"), pairs)


def across_x(v):
    return lax.ppermute(v, "x", [(x, (x + 2) % NX) for x in range(NX)])


def from_wide(v, sign):
    return lax.ppermute(
        v, WIDE, [((i + (2 * sign if i % 2 == 0 else -2 * sign)) % NW, i) for i in range(NW)]
    )


def swap_core(v):
    return lax.ppermute(v, "c", [(0, 1), (1, 0)])


def prep_kernel(emb_ref, seed_ref, ids_ref, two_ref, one_ref, full_ref):
    for block in range(BLK):
        values = emb_ref[block].astype(F32)
        total = jnp.sum(values * values, axis=-1, keepdims=True)
        unit = (values * lax.rsqrt(total + EPS)).astype(BF16)
        full_ref[block * ROWS : (block + 1) * ROWS] = unit
        full_ref[BLK * ROWS :, block * ROWS : (block + 1) * ROWS] = seed_ref[block].astype(BF16)
        if block < 2:
            two_ref[block * D : (block + 1) * D] = jnp.transpose(unit)
        else:
            one_ref[:D] = jnp.transpose(unit)
    two_ref[2 * D :] = ids_ref[...]
    one_ref[D:] = ids_ref[...]


def prepare(embeddings, seeds_t, ids):
    return pl.pallas_call(
        prep_kernel,
        out_shape=(
            jax.ShapeDtypeStruct((2 * D + IDS, ROWS), BF16),
            jax.ShapeDtypeStruct((D + IDS, ROWS), BF16),
            jax.ShapeDtypeStruct((BLK * ROWS + CH, D), BF16),
        ),
        in_specs=[VM, VM, VM],
        out_specs=(VM, VM, VM),
        compiler_params=pltpu.CompilerParams(vmem_limit_bytes=8 << 20),
        cost_estimate=CHEAP,
        name="prep",
    )(embeddings, seeds_t, ids)


def split_ids(neighbours):
    shown = neighbours + 1
    parts = jnp.concatenate([shown >> 4, shown & 15], axis=1).astype(BF16)
    return jnp.pad(parts, ((0, IDS - BLK), (0, ROWS - 2 * NBR)))


def joined_ids(rows):
    parts = rows[-IDS:][:BLK].astype(jnp.int32)
    return parts[:, :NBR] * 16 + parts[:, NBR : 2 * NBR] - 1


def coded(ids, wide, x):
    core = wide & 1
    device = ids // BLK
    step = (device // NX - wide + 2) & (NW - 1)
    first = 4 - 4 * core
    source = jnp.where(
        step == 2,
        0,
        jnp.where(step == 3 - 2 * core, 1, jnp.where(step == first, 2, jnp.where(step == 4 - first, 3, 4))),
    )
    adds = jnp.where(source < 2, 1, jnp.where(source < 4, 1 << STEP, 1 << (2 * STEP)))
    hit = (ids >= 0) & (device % NX == x)
    return jnp.where(hit, source * BLK + ids % BLK + 16 * adds, 0)


def plan_kernel(groups, *refs):
    code_refs = refs[: len(groups)]
    old_ref, list_ref = (refs[-2], refs[-1]) if len(refs) > len(groups) + 1 else (None, refs[-1])
    counts = [jnp.int32(0)] * CHUNKS
    if old_ref is not None:

        def copy(k, _):
            list_ref[k] = old_ref[k]
            return 0

        counts = [old_ref[TOTALS + c] for c in range(CHUNKS)]
        for c in range(2, CHUNKS):
            lax.fori_loop(FIRST[c], FIRST[c] + counts[c], copy, 0)
    for c in range(CHUNKS):
        list_ref[BEFORE + c] = counts[c]
    for ref, group in zip(code_refs, groups):
        for i in range(BLK):
            row = group * BLK + i
            chunks = (0, 1, 4) if row in SOON else (2, 3, 4)

            def body(k, packed, ref=ref, i=i, row=row, chunks=chunks):
                value = ref[i, k]
                entry = row * 16 + (value & 15)
                list_ref[FIRST[chunks[0]] + (packed & ((1 << STEP) - 1))] = entry
                list_ref[FIRST[chunks[1]] + ((packed >> STEP) & ((1 << STEP) - 1))] = entry
                list_ref[FIRST[chunks[2]] + (packed >> (2 * STEP))] = entry
                return packed + (value >> 4)

            packed = sum(counts[c] << (at * STEP) for at, c in enumerate(chunks))
            packed = lax.fori_loop(0, NBR, body, packed, unroll=8)
            for at, c in enumerate(chunks):
                counts[c] = (packed >> (at * STEP)) & ((1 << STEP) - 1)
    for c in range(CHUNKS):
        for pad in range(4):
            list_ref[FIRST[c] + counts[c] + pad] = SPARE * 16 + BASE[c]
        list_ref[COUNTS + c] = (counts[c] + 3) >> 2
        list_ref[TOTALS + c] = counts[c]


def make_plan(groups, codes, old=None):
    operands = [*codes] + ([old] if old is not None else [])
    return pl.pallas_call(
        functools.partial(plan_kernel, groups),
        out_shape=jax.ShapeDtypeStruct((LISTS,), jnp.int32),
        in_specs=[SM] * len(operands),
        out_specs=SM,
        compiler_params=pltpu.CompilerParams(vmem_limit_bytes=1 << 20),
        cost_estimate=LONG,
        name="plan",
    )(*operands)


def tiles(chunk, list_ref, row_ref, col_ref, state_ref, w_ref, sum_ref, base=0):
    steps = list_ref[COUNTS + chunk]

    def four_tiles(step, _):
        for k in range(4):
            n = 4 * step + k
            named = list_ref[FIRST[chunk] + n]
            row, col = named >> 4, (named & 15) - base
            place = jnp.where(row == SPARE, 0, row) * D
            cosine = jnp.dot(
                col_ref[pl.ds(pl.multiple_of(col * ROWS, ROWS), ROWS), :],
                row_ref[pl.ds(pl.multiple_of(place, D), D), :],
                preferred_element_type=F32,
            )
            weight = jnp.exp2(cosine * SCALE)
            w_ref[n] = weight.astype(BF16)
            sum_ref[row, CH:] += jnp.sum(weight.reshape(ROWS // 8, 8, ROWS), axis=0)
        return 0

    def four_spreads(step, _):
        for k in range(4):
            n = 4 * step + k
            named = list_ref[FIRST[chunk] + n]
            sum_ref[named >> 4, :CH] += jnp.dot(
                state_ref[(named & 15) - base], w_ref[n], preferred_element_type=F32
            )
        return 0

    lax.fori_loop(0, steps, four_tiles, 0)
    lax.fori_loop(0, steps, four_spreads, 0)


def put_rows(buf, refs, places):
    for ref, (at, n) in zip(refs, places):
        buf[at * D : (at + n) * D] = ref[: n * D]


def put_cols(buf, states, refs):
    for at, ref in enumerate(refs):
        buf[at * BLK * ROWS : (at + 1) * BLK * ROWS] = ref[: BLK * ROWS]
        for j in range(BLK):
            states[at * BLK + j] = ref[BLK * ROWS :, j * ROWS : (j + 1) * ROWS]


def build_0(list_ref, r0, r1, r2, r3, c0, c1, w_ref, sum_ref, rows, cols, states):
    put_rows(rows, (r0, r1, r2, r3), ((0, 2), (2, 1), (3, 2), (8, 1)))
    put_cols(cols, states, (c0, c1))
    sum_ref[...] = jnp.zeros_like(sum_ref)
    tiles(0, list_ref, rows, cols, states, w_ref, sum_ref)


def build_1(list_ref, rows, c0, c1, c2, c3, given, w_ref, sum_ref, cols, states):
    put_cols(cols, states, (c0, c1, c2, c3))
    sum_ref[...] = given[...]
    tiles(1, list_ref, rows, cols, states, w_ref, sum_ref)


def build_2(list_ref, old_rows, r0, r1, r2, r3, cols, states, given, w2_ref, w3_ref, sum_ref, rows):
    rows[: 5 * D] = old_rows[: 5 * D]
    rows[8 * D : 9 * D] = old_rows[8 * D :]
    put_rows(rows, (r0, r1, r2, r3), ((5, 1), (6, 2), (9, 2), (11, 1)))
    sum_ref[...] = given[...]
    tiles(2, list_ref, rows, cols, states, w2_ref, sum_ref)
    tiles(3, list_ref, rows, cols, states, w3_ref, sum_ref)


def build_3(list_ref, rows, c4, given, w_ref, *refs):
    outs, (sums, states) = refs[:NX], refs[NX:]
    sums[...] = given[...]
    for j in range(BLK):
        states[j] = c4[BLK * ROWS :, j * ROWS : (j + 1) * ROWS]
    tiles(4, list_ref, rows, c4, states, w_ref, sums, base=BASE[4])
    for at, ref in enumerate(outs):
        ref[...] = sums[at * BLK : (at + 1) * BLK]


def build(kernel, room, outs, scratch, *operands):
    return pl.pallas_call(
        kernel,
        out_shape=[jax.ShapeDtypeStruct(*o) for o in outs],
        in_specs=[SM if o.dtype == jnp.int32 else VM for o in operands],
        out_specs=[VM] * len(outs),
        scratch_shapes=[pltpu.VMEM(*s) for s in scratch],
        compiler_params=pltpu.CompilerParams(vmem_limit_bytes=room << 20),
        cost_estimate=LONG,
        name=kernel.__name__,
    )(*operands)


WEIGHTS = ((CAP, ROWS, ROWS), BF16)


def rows_of(n):
    return ((n * D, ROWS), BF16)


def columns(n):
    return [((n * BLK * ROWS, D), BF16), ((n * BLK, CH, ROWS), BF16)]


SUM_BUF = ((SPARE + 1, SUMS, ROWS), F32)


def add_spread(chunk, list_ref, w_ref, state_ref, sum_ref, low, high):
    def four(step, _):
        for k in range(4):
            n = low + 4 * step + k
            named = list_ref[FIRST[chunk] + n]
            row = jnp.where(n < high, named >> 4, SPARE)
            sum_ref[row] += jnp.dot(state_ref[named & 15], w_ref[n], preferred_element_type=F32)
        return 0

    lax.fori_loop(0, (high - low + 3) >> 2, four, 0)


def spread_near(near_ref, list_ref, w0, w2, s0, s1, sum_ref, states):
    sum_ref[...] = jnp.zeros_like(sum_ref)
    for at, ref in enumerate((s0, s1)):
        states[at * BLK : (at + 1) * BLK] = ref[...]
    add_spread(0, near_ref, w0, states, sum_ref, 0, near_ref[TOTALS])
    add_spread(2, list_ref, w2, states, sum_ref, 0, list_ref[TOTALS + 2])


def spread_far(list_ref, w3, w4, s2, s3, s4, given, far, sums, states):
    sums[...] = given[...]
    for at, ref in enumerate((s2, s3, s4)):
        states[(at + 2) * BLK : (at + 3) * BLK] = ref[...]
    for chunk, w_ref in ((3, w3), (4, w4)):
        add_spread(chunk, list_ref, w_ref, states, sums, list_ref[BEFORE + chunk], list_ref[TOTALS + chunk])
    far[...] = sums[3 * BLK : SPARE]


def spread_rest(near_ref, list_ref, w1, w3, w4, s2, s3, s4, given, own, back, fore, sums, states):
    sums[...] = given[...]
    for at, ref in enumerate((s2, s3, s4)):
        states[(at + 2) * BLK : (at + 3) * BLK] = ref[...]
    add_spread(1, near_ref, w1, states, sums, 0, near_ref[TOTALS + 1])
    for chunk, w_ref in ((3, w3), (4, w4)):
        add_spread(chunk, list_ref, w_ref, states, sums, 0, list_ref[BEFORE + chunk])
    for at, ref in enumerate((own, back, fore)):
        ref[...] = sums[at * BLK : (at + 1) * BLK]


def spread(lists, weights, states):
    sums = ((SPARE + 1, CH, ROWS), F32)
    held = ((5 * BLK, CH, ROWS), BF16)
    part = ((BLK, CH, ROWS), F32)
    w0, w1, w2, w3, w4 = weights
    (near,) = build(spread_near, 3, [sums], [held], *lists, w0, w2, *states[:2])
    (far,) = build(spread_far, 4, [part], [sums, held], lists[1], w3, w4, *states[2:], near)
    near, _ = lax.optimization_barrier((near, far))
    return *build(
        spread_rest, 4, [part] * (NX - 1), [sums, held], *lists, w1, w3, w4, *states[2:], near
    ), far


def wide_exchange(v):
    one = from_wide(v, 1)
    partner = swap_core(v)
    other = from_wide(v, -1)
    across = swap_core(one)
    return [v, partner, one, other, across]


def reduce_rows(own, back, fore, far):
    first = lax.optimization_barrier(own + across_x(far))
    return first + along_x(back, -1) + along_x(fore, 1)


def local(embeddings, seeds, neighbours):
    code = functools.partial(coded, wide=lax.axis_index(WIDE), x=lax.axis_index("x"))
    seeds_t = jnp.swapaxes(seeds, 1, 2)
    after = lambda v, *done: lax.optimization_barrier((v, *done))[0]
    two, one, full = prepare(embeddings, seeds_t, split_ids(neighbours))
    back_two = along_x(two, 1)
    fore_one = along_x(one, -1)
    above = from_wide(full, 1)
    below = from_wide(full, -1)
    back_one = along_x(one, 1)
    back_two, fore_one, back_one, late_full, late_two = lax.optimization_barrier(
        (back_two, fore_one, back_one, full, two)
    )
    partner = swap_core(late_full)
    far_two = along_x(back_two, 1)
    fore_two = along_x(late_two, -1)
    far_one = along_x(after(fore_one, partner), -1)

    near = make_plan(
        (0, 1, 2), [code(neighbours), code(joined_ids(back_two)), code(joined_ids(fore_one))]
    )
    w0, sums, rows = build(
        build_0, 6, [WEIGHTS, SUM_BUF, rows_of(9)], columns(2),
        near, two, one, back_two, fore_one, full, partner,
    )
    beside = swap_core(after(above, sums))
    w1, sums, cols, states = build(
        build_1, 4, [WEIGHTS, SUM_BUF, *columns(4)], [], near, rows, full, partner, above, below, sums
    )
    lists = make_plan((3,), [code(joined_ids(after(far_two, sums)))], near)
    w2, w3, sums, rows = build(
        build_2, 4, [WEIGHTS, WEIGHTS, SUM_BUF, rows_of(12)], [],
        lists, rows, back_one, fore_two, far_two, far_one, cols, states, sums,
    )
    w4, own, back, fore, far = build(
        build_3, 4, [WEIGHTS] + [((BLK, SUMS, ROWS), F32)] * NX, [SUM_BUF, ((BLK, CH, ROWS), BF16)],
        lists, rows, beside, sums,
    )
    lists = [near, lists]
    weights = [w0, w1, w2, w3, w4]

    total = reduce_rows(own, back, fore, far)
    scale = ALPHA / jnp.sum(total[:, CH:], axis=1, keepdims=True)
    prior = (1.0 - ALPHA) * seeds_t
    scores = total[:, :CH] * scale + prior
    for _ in range(ITERS - 1):
        states = wide_exchange(scores.astype(BF16))
        total = reduce_rows(*spread(lists, weights, states))
        scores = total * scale + prior
    return jnp.swapaxes(scores, 1, 2)


def solution(mesh):
    fine = Mesh(mesh.devices.reshape(4, 4, 2, 4), ("z", "y", "c", "x"))
    everywhere = ("z", "y", "c", "x")
    return jax.shard_map(
        local,
        mesh=fine,
        in_specs=(P(everywhere, None, None), P(everywhere, None, None), P(everywhere, None)),
        out_specs=P(everywhere, None, None),
        check_vma=False,
    )
```

```python
import functools
import math

import jax
import jax.numpy as jnp
from jax import lax
from jax.experimental import pallas as pl
from jax.experimental.pallas import tpu as pltpu
from jax.sharding import Mesh, PartitionSpec as P

NBR = 32
ITERS = 3
SHARP = 24.0
ALPHA = 0.8
EPS = 1e-06
ROWS = 256
D = 768
CH = 64
BLK = 3
NX = 4
NW = 32
SCALE = SHARP * math.log2(math.e)
WIDE = ("z", "y", "c")
VM = pl.BlockSpec(memory_space=pltpu.VMEM)
SM = pl.BlockSpec(memory_space=pltpu.SMEM)
F32 = jnp.float32
BF16 = jnp.bfloat16
FIRST = (0, 48, 96, 144, 192)
CAPS = (44, 44, 36, 36, 40)
BASE = (0, 6, 0, 6, 12)
CHUNKS = 5
SOON = (0, 1, 2, 3, 4, 5, 8)
TOTALS = 245
BEFORE = 250
LISTS = 256
STEP = 9
SPARE = NX * BLK
SUMS = CH + 8
IDS = 16
CHEAP = pl.CostEstimate(flops=1000, bytes_accessed=1000, transcendentals=0)
LONG = pl.CostEstimate(flops=30_000_000_000, bytes_accessed=1000, transcendentals=0)


def along_x(v, sign):
    pairs = []
    for core in range(2):
        by = sign if core == 0 else -sign
        pairs += [(core * NX + x, core * NX + (x + by) % NX) for x in range(NX)]
    return lax.ppermute(v, ("c", "x"), pairs)


def across_x(v):
    return lax.ppermute(v, "x", [(x, (x + 2) % NX) for x in range(NX)])


def from_wide(v, sign):
    return lax.ppermute(
        v, WIDE, [((i + (2 * sign if i % 2 == 0 else -2 * sign)) % NW, i) for i in range(NW)]
    )


def swap_core(v):
    return lax.ppermute(v, "c", [(0, 1), (1, 0)])


def prep_kernel(emb_hbm, seed_hbm, ids_ref, two_ref, full_ref, emb_buf, seed_buf, sems):
    copies = [pltpu.make_async_copy(emb_hbm.at[b], emb_buf.at[b], sems.at[b]) for b in range(BLK)]
    copies.append(pltpu.make_async_copy(seed_hbm, seed_buf, sems.at[BLK]))
    for copy in copies:
        copy.start()
    for block in range(BLK):
        copies[block].wait()
        values = emb_buf[block].astype(F32)
        total = jnp.sum(values * values, axis=-1, keepdims=True)
        unit = (values * lax.rsqrt(total + EPS)).astype(BF16)
        full_ref[block * ROWS : (block + 1) * ROWS] = unit
        if block < 2:
            two_ref[block * D : (block + 1) * D] = jnp.transpose(unit)
    two_ref[2 * D :] = ids_ref[...]
    copies[BLK].wait()
    for block in range(BLK):
        full_ref[BLK * ROWS :, block * ROWS : (block + 1) * ROWS] = seed_buf[block].astype(BF16)


def prepare(embeddings, seeds_t, ids):
    far = pl.BlockSpec(memory_space=pltpu.HBM)
    return pl.pallas_call(
        prep_kernel,
        out_shape=(
            jax.ShapeDtypeStruct((2 * D + IDS, ROWS), BF16),
            jax.ShapeDtypeStruct((BLK * ROWS + CH, D), BF16),
        ),
        in_specs=[far, far, VM],
        out_specs=(VM, VM),
        scratch_shapes=[
            pltpu.VMEM((BLK, ROWS, D), BF16),
            pltpu.VMEM((BLK, CH, ROWS), F32),
            pltpu.SemaphoreType.DMA((BLK + 1,)),
        ],
        compiler_params=pltpu.CompilerParams(vmem_limit_bytes=8 << 20),
        cost_estimate=CHEAP,
        name="prep",
    )(
        pltpu.with_memory_space_constraint(embeddings, pltpu.HBM),
        pltpu.with_memory_space_constraint(seeds_t, pltpu.HBM),
        ids,
    )


def third_kernel(full_ref, ids_ref, one_ref):
    one_ref[:D] = jnp.transpose(full_ref[2 * ROWS : BLK * ROWS])
    one_ref[D:] = ids_ref[...]


def third_turned(full, ids):
    return pl.pallas_call(
        third_kernel,
        out_shape=jax.ShapeDtypeStruct((D + IDS, ROWS), BF16),
        in_specs=[VM, VM],
        out_specs=VM,
        compiler_params=pltpu.CompilerParams(vmem_limit_bytes=2 << 20),
        cost_estimate=LONG,
        name="third",
    )(full, ids)


def split_ids(neighbours):
    shown = neighbours + 1
    parts = jnp.concatenate([shown >> 4, shown & 15], axis=1).astype(BF16)
    return jnp.pad(parts, ((0, IDS - BLK), (0, ROWS - 2 * NBR)))


def joined_ids(rows):
    parts = rows[-IDS:][:BLK].astype(jnp.int32)
    return parts[:, :NBR] * 16 + parts[:, NBR : 2 * NBR] - 1


def coded(ids, wide, x):
    core = wide & 1
    device = ids // BLK
    step = (device // NX - wide + 2) & (NW - 1)
    first = 4 - 4 * core
    source = jnp.where(
        step == 2,
        0,
        jnp.where(step == 3 - 2 * core, 1, jnp.where(step == first, 2, jnp.where(step == 4 - first, 3, 4))),
    )
    adds = jnp.where(source < 2, 1, jnp.where(source < 4, 1 << STEP, 1 << (2 * STEP)))
    hit = (ids >= 0) & (device % NX == x)
    return jnp.where(hit, source * BLK + ids % BLK + 16 * adds, 0)


def plan_kernel(groups, *refs):
    code_refs = refs[: len(groups)]
    old_ref, list_ref = (refs[-2], refs[-1]) if len(refs) > len(groups) + 1 else (None, refs[-1])
    counts = [jnp.int32(0)] * CHUNKS
    if old_ref is not None:

        def copy(k, _):
            list_ref[k] = old_ref[k]
            return 0

        counts = [old_ref[TOTALS + c] for c in range(CHUNKS)]
        for c in range(2, CHUNKS):
            lax.fori_loop(FIRST[c], FIRST[c] + counts[c], copy, 0)
    for c in range(CHUNKS):
        list_ref[BEFORE + c] = counts[c]
    for ref, group in zip(code_refs, groups):
        for i in range(BLK):
            row = group * BLK + i
            chunks = (0, 1, 4) if row in SOON else (2, 3, 4)

            def body(k, packed, ref=ref, i=i, row=row, chunks=chunks):
                value = ref[i, k]
                entry = row * 16 + (value & 15)
                list_ref[FIRST[chunks[0]] + (packed & ((1 << STEP) - 1))] = entry
                list_ref[FIRST[chunks[1]] + ((packed >> STEP) & ((1 << STEP) - 1))] = entry
                list_ref[FIRST[chunks[2]] + (packed >> (2 * STEP))] = entry
                return packed + (value >> 4)

            packed = sum(counts[c] << (at * STEP) for at, c in enumerate(chunks))
            packed = lax.fori_loop(0, NBR, body, packed, unroll=8)
            for at, c in enumerate(chunks):
                counts[c] = (packed >> (at * STEP)) & ((1 << STEP) - 1)
    for c in range(CHUNKS):
        for pad in range(4):
            list_ref[FIRST[c] + counts[c] + pad] = SPARE * 16 + BASE[c]
        list_ref[TOTALS + c] = counts[c]


def make_plan(groups, codes, old=None):
    operands = [*codes] + ([old] if old is not None else [])
    return pl.pallas_call(
        functools.partial(plan_kernel, groups),
        out_shape=jax.ShapeDtypeStruct((LISTS,), jnp.int32),
        in_specs=[SM] * len(operands),
        out_specs=SM,
        compiler_params=pltpu.CompilerParams(vmem_limit_bytes=1 << 20),
        cost_estimate=LONG,
        name="plan",
    )(*operands)


def tiles(chunk, list_ref, row_ref, col_ref, state_ref, w_ref, sum_ref, low=0, high=None, base=0):
    high = list_ref[TOTALS + chunk] if high is None else high
    steps = (high - low + 3) >> 2

    def spread_four(step, live):
        for k in range(4):
            n = low + 4 * step + k
            named = list_ref[FIRST[chunk] + n]
            row = jnp.where(live & (n < high), named >> 4, SPARE)
            sum_ref[row, :CH] += jnp.dot(
                state_ref[(named & 15) - base], w_ref[n], preferred_element_type=F32
            )

    def four_tiles(step, _):
        spread_four(jnp.maximum(step - 1, 0), step > 0)
        for k in range(4):
            n = low + 4 * step + k
            named = list_ref[FIRST[chunk] + n]
            row, col = jnp.where(n < high, named >> 4, SPARE), (named & 15) - base
            place = jnp.where(row == SPARE, 0, row) * D
            cosine = jnp.dot(
                col_ref[pl.ds(pl.multiple_of(col * ROWS, ROWS), ROWS), :],
                row_ref[pl.ds(pl.multiple_of(place, D), D), :],
                preferred_element_type=F32,
            )
            weight = jnp.exp2(cosine * SCALE)
            w_ref[n] = weight.astype(BF16)
            sum_ref[row, CH:] += jnp.sum(weight.reshape(ROWS // 8, 8, ROWS), axis=0)
        return 0

    lax.fori_loop(0, steps, four_tiles, 0)
    spread_four(jnp.maximum(steps - 1, 0), steps > 0)


def put_rows(buf, refs, places):
    for ref, (at, n) in zip(refs, places):
        buf[at * D : (at + n) * D] = ref[: n * D]


def put_cols(buf, states, refs):
    for at, ref in enumerate(refs):
        buf[at * BLK * ROWS : (at + 1) * BLK * ROWS] = ref[: BLK * ROWS]
        for j in range(BLK):
            states[at * BLK + j] = ref[BLK * ROWS :, j * ROWS : (j + 1) * ROWS]


def build_0(list_ref, r0, r1, r2, r3, r4, c0, c1, w_ref, sum_ref, rows, cols, states):
    put_rows(rows, (r0, r1, r2, r3, r4), ((0, 2), (2, 1), (3, 2), (5, 1), (8, 1)))
    put_cols(cols, states, (c0, c1))
    sum_ref[...] = jnp.zeros_like(sum_ref)
    tiles(0, list_ref, rows, cols, states, w_ref, sum_ref)


def build_1(list_ref, rows, c0, c1, c2, c3, given, w_ref, sum_ref, cols, states):
    put_cols(cols, states, (c0, c1, c2, c3))
    sum_ref[...] = given[...]
    tiles(1, list_ref, rows, cols, states, w_ref, sum_ref)


def build_2(list_ref, old_rows, r0, r1, r2, cols, states, given, w2_ref, w3_ref, sum_ref, rows):
    rows[: 6 * D] = old_rows[: 6 * D]
    rows[8 * D : 9 * D] = old_rows[8 * D :]
    put_rows(rows, (r0, r1, r2), ((6, 2), (9, 2), (11, 1)))
    sum_ref[...] = given[...]
    tiles(2, list_ref, rows, cols, states, w2_ref, sum_ref)
    tiles(3, list_ref, rows, cols, states, w3_ref, sum_ref)


def last_columns(list_ref, rows, c4, given, w_ref, outs, sums, states, first, low, high):
    sums[...] = given[...]
    for j in range(BLK):
        states[j] = c4[BLK * ROWS :, j * ROWS : (j + 1) * ROWS]
    tiles(4, list_ref, rows, c4, states, w_ref, sums, low, high, BASE[4])
    for at, ref in enumerate(outs):
        ref[...] = sums[(first + at) * BLK : (first + at + 1) * BLK]


def build_far(list_ref, rows, c4, given, w_ref, far, sums, states):
    last_columns(
        list_ref, rows, c4, given, w_ref, (far,), sums, states, 3, list_ref[BEFORE + 4], list_ref[TOTALS + 4]
    )


def build_rest(list_ref, rows, c4, given, w_ref, own, back, fore, sums, states):
    last_columns(
        list_ref, rows, c4, given, w_ref, (own, back, fore), sums, states, 0, 0, list_ref[BEFORE + 4]
    )


def build(kernel, room, outs, scratch, *operands, cost=None):
    return pl.pallas_call(
        kernel,
        out_shape=[jax.ShapeDtypeStruct(*o) for o in outs],
        in_specs=[SM if o.dtype == jnp.int32 else VM for o in operands],
        out_specs=[VM] * len(outs),
        scratch_shapes=[pltpu.VMEM(*s) for s in scratch],
        compiler_params=pltpu.CompilerParams(vmem_limit_bytes=room << 20),
        cost_estimate=cost or LONG,
        name=kernel.__name__,
    )(*operands)


def weights_of(chunk):
    return ((CAPS[chunk], ROWS, ROWS), BF16)


def rows_of(n):
    return ((n * D, ROWS), BF16)


def columns(n):
    return [((n * BLK * ROWS, D), BF16), ((n * BLK, CH, ROWS), BF16)]


SUM_BUF = ((SPARE + 1, SUMS, ROWS), F32)


def add_spread(chunk, list_ref, w_ref, state_ref, sum_ref, low, high):
    def four(step, _):
        for k in range(4):
            n = low + 4 * step + k
            named = list_ref[FIRST[chunk] + n]
            row = jnp.where(n < high, named >> 4, SPARE)
            sum_ref[row] += jnp.dot(state_ref[named & 15], w_ref[n], preferred_element_type=F32)
        return 0

    lax.fori_loop(0, (high - low + 3) >> 2, four, 0)


def spread_near(near_ref, list_ref, w0, w2, s0, s1, sum_ref, states):
    sum_ref[...] = jnp.zeros_like(sum_ref)
    for at, ref in enumerate((s0, s1)):
        states[at * BLK : (at + 1) * BLK] = ref[...]
    add_spread(0, near_ref, w0, states, sum_ref, 0, near_ref[TOTALS])
    add_spread(2, list_ref, w2, states, sum_ref, 0, list_ref[TOTALS + 2])


def spread_far(list_ref, w3, w4, s2, s3, s4, given, far, sums, states):
    sums[...] = given[...]
    for at, ref in enumerate((s2, s3, s4)):
        states[(at + 2) * BLK : (at + 3) * BLK] = ref[...]
    for chunk, w_ref in ((3, w3), (4, w4)):
        add_spread(chunk, list_ref, w_ref, states, sums, list_ref[BEFORE + chunk], list_ref[TOTALS + chunk])
    far[...] = sums[3 * BLK : SPARE]


def spread_rest(near_ref, list_ref, w1, w3, w4, s2, s3, s4, given, own, back, fore, sums, states):
    sums[...] = given[...]
    for at, ref in enumerate((s2, s3, s4)):
        states[(at + 2) * BLK : (at + 3) * BLK] = ref[...]
    add_spread(1, near_ref, w1, states, sums, 0, near_ref[TOTALS + 1])
    for chunk, w_ref in ((3, w3), (4, w4)):
        add_spread(chunk, list_ref, w_ref, states, sums, 0, list_ref[BEFORE + chunk])
    for at, ref in enumerate((own, back, fore)):
        ref[...] = sums[at * BLK : (at + 1) * BLK]


def spread(lists, weights, states):
    sums = ((SPARE + 1, CH, ROWS), F32)
    held = ((5 * BLK, CH, ROWS), BF16)
    part = ((BLK, CH, ROWS), F32)
    w0, w1, w2, w3, w4_far, w4 = weights
    (near,) = build(spread_near, 3, [sums], [held], *lists, w0, w2, *states[:2])
    (far,) = build(spread_far, 4, [part], [sums, held], lists[1], w3, w4_far, *states[2:], near)
    near, _ = lax.optimization_barrier((near, far))
    return *build(
        spread_rest, 4, [part] * (NX - 1), [sums, held], *lists, w1, w3, w4, *states[2:], near
    ), far


def wide_exchange(v):
    one = from_wide(v, 1)
    partner = swap_core(v)
    other = from_wide(v, -1)
    across = swap_core(one)
    return [v, partner, one, other, across]


def reduce_rows(own, back, fore, far):
    first = lax.optimization_barrier(own + across_x(far))
    return first + along_x(back, -1) + along_x(fore, 1)


def local(embeddings, seeds, neighbours):
    code = functools.partial(coded, wide=lax.axis_index(WIDE), x=lax.axis_index("x"))
    seeds_t = jnp.swapaxes(seeds, 1, 2)
    after = lambda v, *done: lax.optimization_barrier((v, *done))[0]
    ids = split_ids(neighbours)
    two, full = prepare(embeddings, seeds_t, ids)
    one = third_turned(full, ids)
    back_two = along_x(two, 1)
    above = from_wide(full, 1)
    below = from_wide(full, -1)
    fore_one = along_x(one, -1)
    back_one = along_x(one, 1)
    back_two, fore_one, back_one, late_full, late_two = lax.optimization_barrier(
        (back_two, fore_one, back_one, full, two)
    )
    partner = swap_core(late_full)
    far_two = along_x(back_two, 1)
    fore_two = along_x(late_two, -1)
    far_one = along_x(after(fore_one, partner), -1)

    near = make_plan(
        (0, 1, 2), [code(neighbours), code(joined_ids(back_two)), code(joined_ids(fore_one))]
    )
    w0, sums, rows = build(
        build_0, 6, [weights_of(0), SUM_BUF, rows_of(9)], columns(2),
        near, two, one, back_two, back_one, fore_one, full, partner,
    )
    beside = swap_core(after(above, sums))
    w1, sums, cols, states = build(
        build_1, 4, [weights_of(1), SUM_BUF, *columns(4)], [],
        near, rows, full, partner, above, below, sums,
    )
    lists = make_plan((3,), [code(joined_ids(after(far_two, sums)))], near)
    w2, w3, sums, rows = build(
        build_2, 4, [weights_of(2), weights_of(3), SUM_BUF, rows_of(12)], [],
        lists, rows, fore_two, far_two, far_one, cols, states, sums,
    )
    part = ((BLK, SUMS, ROWS), F32)
    scratch = [SUM_BUF, ((BLK, CH, ROWS), BF16)]
    w4_far, far = build(build_far, 4, [weights_of(4), part], scratch, lists, rows, beside, sums)
    w4, own, back, fore = build(
        build_rest, 4, [weights_of(4)] + [part] * (NX - 1), scratch,
        lists, rows, beside, after(sums, far),
    )
    lists = [near, lists]
    weights = [w0, w1, w2, w3, w4_far, w4]

    total = reduce_rows(own, back, fore, far)
    scale = ALPHA / jnp.sum(total[:, CH:], axis=1, keepdims=True)
    prior = (1.0 - ALPHA) * seeds_t
    scores = total[:, :CH] * scale + prior
    for _ in range(ITERS - 1):
        states = wide_exchange(scores.astype(BF16))
        total = reduce_rows(*spread(lists, weights, states))
        scores = total * scale + prior
    return jnp.swapaxes(scores, 1, 2)


def solution(mesh):
    fine = Mesh(mesh.devices.reshape(4, 4, 2, 4), ("z", "y", "c", "x"))
    everywhere = ("z", "y", "c", "x")
    return jax.shard_map(
        local,
        mesh=fine,
        in_specs=(P(everywhere, None, None), P(everywhere, None, None), P(everywhere, None)),
        out_specs=P(everywhere, None, None),
        check_vma=False,
    )
```

```python
import functools
import math

import jax
import jax.numpy as jnp
from jax import lax
from jax.experimental import pallas as pl
from jax.experimental.pallas import tpu as pltpu
from jax.sharding import Mesh, PartitionSpec as P

NBR = 32
ITERS = 3
SHARP = 24.0
ALPHA = 0.8
EPS = 1e-06
ROWS = 256
D = 768
CH = 64
BLK = 3
NX = 4
NW = 32
SCALE = SHARP * math.log2(math.e)
WIDE = ("z", "y", "c")
VM = pl.BlockSpec(memory_space=pltpu.VMEM)
SM = pl.BlockSpec(memory_space=pltpu.SMEM)
F32 = jnp.float32
BF16 = jnp.bfloat16
FIRST = (0, 48, 96, 144, 192)
CAPS = (44, 44, 36, 36, 40)
BASE = (0, 6, 0, 6, 12)
CHUNKS = 5
SOON = (0, 1, 2, 3, 4, 5, 8)
TOTALS = 245
BEFORE = 250
LISTS = 256
STEP = 9
CODED = 32000.0
SPARE = NX * BLK
SUMS = CH + 8
IDS = 16
CHEAP = pl.CostEstimate(flops=1000, bytes_accessed=1000, transcendentals=0)
LONG = pl.CostEstimate(flops=30_000_000_000, bytes_accessed=1000, transcendentals=0)


def along_x(v, sign):
    pairs = []
    for core in range(2):
        by = sign if core == 0 else -sign
        pairs += [(core * NX + x, core * NX + (x + by) % NX) for x in range(NX)]
    return lax.ppermute(v, ("c", "x"), pairs)


def across_x(v):
    return lax.ppermute(v, "x", [(x, (x + 2) % NX) for x in range(NX)])


def from_wide(v, sign):
    return lax.ppermute(
        v, WIDE, [((i + (2 * sign if i % 2 == 0 else -2 * sign)) % NW, i) for i in range(NW)]
    )


def swap_core(v):
    return lax.ppermute(v, "c", [(0, 1), (1, 0)])


def prep_kernel(emb_hbm, seed_hbm, ids_ref, two_ref, full_ref, emb_buf, seed_buf, sems):
    copies = [pltpu.make_async_copy(emb_hbm.at[b], emb_buf.at[b], sems.at[b]) for b in range(BLK)]
    copies.append(pltpu.make_async_copy(seed_hbm, seed_buf, sems.at[BLK]))
    for copy in copies:
        copy.start()
    for block in range(BLK):
        copies[block].wait()
        values = emb_buf[block].astype(F32)
        total = jnp.sum(values * values, axis=-1, keepdims=True)
        unit = (values * lax.rsqrt(total + EPS)).astype(BF16)
        full_ref[block * ROWS : (block + 1) * ROWS] = unit
        if block < 2:
            two_ref[block * D : (block + 1) * D] = jnp.transpose(unit)
    two_ref[2 * D :] = ids_ref[...]
    copies[BLK].wait()
    for block in range(BLK):
        full_ref[BLK * ROWS :, block * ROWS : (block + 1) * ROWS] = seed_buf[block].astype(BF16)


def prepare(embeddings, seeds_t, ids):
    far = pl.BlockSpec(memory_space=pltpu.HBM)
    return pl.pallas_call(
        prep_kernel,
        out_shape=(
            jax.ShapeDtypeStruct((2 * D + IDS, ROWS), BF16),
            jax.ShapeDtypeStruct((BLK * ROWS + CH, D), BF16),
        ),
        in_specs=[far, far, VM],
        out_specs=(VM, VM),
        scratch_shapes=[
            pltpu.VMEM((BLK, ROWS, D), BF16),
            pltpu.VMEM((BLK, CH, ROWS), F32),
            pltpu.SemaphoreType.DMA((BLK + 1,)),
        ],
        compiler_params=pltpu.CompilerParams(vmem_limit_bytes=8 << 20),
        cost_estimate=CHEAP,
        name="prep",
    )(
        pltpu.with_memory_space_constraint(embeddings, pltpu.HBM),
        pltpu.with_memory_space_constraint(seeds_t, pltpu.HBM),
        ids,
    )


def third_kernel(full_ref, ids_ref, one_ref):
    one_ref[:D] = jnp.transpose(full_ref[2 * ROWS : BLK * ROWS])
    one_ref[D:] = ids_ref[...]


def third_turned(full, ids):
    return pl.pallas_call(
        third_kernel,
        out_shape=jax.ShapeDtypeStruct((D + IDS, ROWS), BF16),
        in_specs=[VM, VM],
        out_specs=VM,
        compiler_params=pltpu.CompilerParams(vmem_limit_bytes=2 << 20),
        cost_estimate=LONG,
        name="third",
    )(full, ids)


def split_ids(neighbours):
    shown = neighbours + 1
    parts = jnp.concatenate([shown >> 4, shown & 15], axis=1).astype(BF16)
    return jnp.pad(parts, ((0, IDS - BLK), (0, ROWS - 2 * NBR)))


def joined_ids(rows):
    parts = rows[-IDS:][:BLK].astype(jnp.int32)
    return parts[:, :NBR] * 16 + parts[:, NBR : 2 * NBR] - 1


def coded(ids, wide, x):
    core = wide & 1
    device = ids // BLK
    step = (device // NX - wide + 2) & (NW - 1)
    first = 4 - 4 * core
    source = jnp.where(
        step == 2,
        0,
        jnp.where(step == 3 - 2 * core, 1, jnp.where(step == first, 2, jnp.where(step == 4 - first, 3, 4))),
    )
    adds = jnp.where(source < 2, 1, jnp.where(source < 4, 1 << STEP, 1 << (2 * STEP)))
    hit = (ids >= 0) & (device % NX == x)
    return jnp.where(hit, source * BLK + ids % BLK + 16 * adds, 0)


def plan_kernel(groups, *refs):
    code_refs = refs[: len(groups)]
    old_ref, list_ref = (refs[-2], refs[-1]) if len(refs) > len(groups) + 1 else (None, refs[-1])
    counts = [jnp.int32(0)] * CHUNKS
    if old_ref is not None:

        def copy(k, _):
            list_ref[k] = old_ref[k]
            return 0

        counts = [old_ref[TOTALS + c] for c in range(CHUNKS)]
        for c in range(2, CHUNKS):
            lax.fori_loop(FIRST[c], FIRST[c] + counts[c], copy, 0)
    for c in range(CHUNKS):
        list_ref[BEFORE + c] = counts[c]
    for ref, group in zip(code_refs, groups):
        for i in range(BLK):
            row = group * BLK + i
            chunks = (0, 1, 4) if row in SOON else (2, 3, 4)

            def body(k, packed, ref=ref, i=i, row=row, chunks=chunks):
                value = ref[i, k]
                entry = row * 16 + (value & 15)
                list_ref[FIRST[chunks[0]] + (packed & ((1 << STEP) - 1))] = entry
                list_ref[FIRST[chunks[1]] + ((packed >> STEP) & ((1 << STEP) - 1))] = entry
                list_ref[FIRST[chunks[2]] + (packed >> (2 * STEP))] = entry
                return packed + (value >> 4)

            packed = sum(counts[c] << (at * STEP) for at, c in enumerate(chunks))
            packed = lax.fori_loop(0, NBR, body, packed, unroll=8)
            for at, c in enumerate(chunks):
                counts[c] = (packed >> (at * STEP)) & ((1 << STEP) - 1)
    for c in range(CHUNKS):
        for pad in range(4):
            list_ref[FIRST[c] + counts[c] + pad] = SPARE * 16 + BASE[c]
        list_ref[TOTALS + c] = counts[c]


def make_plan(groups, codes, old=None):
    operands = [*codes] + ([old] if old is not None else [])
    return pl.pallas_call(
        functools.partial(plan_kernel, groups),
        out_shape=jax.ShapeDtypeStruct((LISTS,), jnp.int32),
        in_specs=[SM] * len(operands),
        out_specs=SM,
        compiler_params=pltpu.CompilerParams(vmem_limit_bytes=1 << 20),
        cost_estimate=LONG,
        name="plan",
    )(*operands)


def tiles(chunk, list_ref, row_ref, col_ref, state_ref, w_ref, sum_ref, low=0, high=None, base=0):
    high = list_ref[TOTALS + chunk] if high is None else high
    steps = (high - low + 3) >> 2

    def spread_four(step, live):
        for k in range(4):
            n = low + 4 * step + k
            named = list_ref[FIRST[chunk] + n]
            row = jnp.where(live & (n < high), named >> 4, SPARE)
            sum_ref[row, :CH] += jnp.dot(
                state_ref[(named & 15) - base], w_ref[n], preferred_element_type=F32
            )

    def four_tiles(step, _):
        spread_four(jnp.maximum(step - 1, 0), step > 0)
        for k in range(4):
            n = low + 4 * step + k
            named = list_ref[FIRST[chunk] + n]
            row, col = jnp.where(n < high, named >> 4, SPARE), (named & 15) - base
            place = jnp.where(row == SPARE, 0, row) * D
            cosine = jnp.dot(
                col_ref[pl.ds(pl.multiple_of(col * ROWS, ROWS), ROWS), :],
                row_ref[pl.ds(pl.multiple_of(place, D), D), :],
                preferred_element_type=F32,
            )
            weight = jnp.exp2(cosine * SCALE)
            w_ref[n] = weight.astype(BF16)
            sum_ref[row, CH:] += jnp.sum(weight.reshape(ROWS // 8, 8, ROWS), axis=0)
        return 0

    lax.fori_loop(0, steps, four_tiles, 0)
    spread_four(jnp.maximum(steps - 1, 0), steps > 0)


def put_rows(buf, refs, places):
    for ref, (at, n) in zip(refs, places):
        buf[at * D : (at + n) * D] = ref[: n * D]


def put_cols(buf, states, refs):
    for at, ref in enumerate(refs):
        buf[at * BLK * ROWS : (at + 1) * BLK * ROWS] = ref[: BLK * ROWS]
        for j in range(BLK):
            states[at * BLK + j] = ref[BLK * ROWS :, j * ROWS : (j + 1) * ROWS]


def build_0(list_ref, r0, r1, r2, r3, r4, c0, c1, w_ref, sum_ref, rows, cols, states):
    put_rows(rows, (r0, r1, r2, r3, r4), ((0, 2), (2, 1), (3, 2), (5, 1), (8, 1)))
    put_cols(cols, states, (c0, c1))
    sum_ref[...] = jnp.zeros_like(sum_ref)
    tiles(0, list_ref, rows, cols, states, w_ref, sum_ref)


def build_1(list_ref, rows, c0, c1, c2, c3, given, w_ref, sum_ref, cols, states):
    put_cols(cols, states, (c0, c1, c2, c3))
    sum_ref[...] = given[...]
    tiles(1, list_ref, rows, cols, states, w_ref, sum_ref)


def build_2(list_ref, old_rows, r0, r1, r2, cols, states, given, w2_ref, w3_ref, sum_ref, rows):
    rows[: 6 * D] = old_rows[: 6 * D]
    rows[8 * D : 9 * D] = old_rows[8 * D :]
    put_rows(rows, (r0, r1, r2), ((6, 2), (9, 2), (11, 1)))
    sum_ref[...] = given[...]
    tiles(2, list_ref, rows, cols, states, w2_ref, sum_ref)
    tiles(3, list_ref, rows, cols, states, w3_ref, sum_ref)


def last_columns(list_ref, rows, c4, given, w_ref, outs, sums, states, first, low, high):
    sums[...] = given[...]
    for j in range(BLK):
        states[j] = c4[BLK * ROWS :, j * ROWS : (j + 1) * ROWS]
    tiles(4, list_ref, rows, c4, states, w_ref, sums, low, high, BASE[4])
    for at, ref in enumerate(outs):
        ref[...] = sums[(first + at) * BLK : (first + at + 1) * BLK]


def build_far(list_ref, rows, c4, given, w_ref, far, sums, states):
    last_columns(
        list_ref, rows, c4, given, w_ref, (far,), sums, states, 3, list_ref[BEFORE + 4], list_ref[TOTALS + 4]
    )


def build_rest(list_ref, rows, c4, given, w_ref, own, back, fore, sums, states):
    last_columns(
        list_ref, rows, c4, given, w_ref, (own, back, fore), sums, states, 0, 0, list_ref[BEFORE + 4]
    )


def build(kernel, room, outs, scratch, *operands, cost=None):
    return pl.pallas_call(
        kernel,
        out_shape=[jax.ShapeDtypeStruct(*o) for o in outs],
        in_specs=[SM if o.dtype == jnp.int32 else VM for o in operands],
        out_specs=[VM] * len(outs),
        scratch_shapes=[pltpu.VMEM(*s) for s in scratch],
        compiler_params=pltpu.CompilerParams(vmem_limit_bytes=room << 20),
        cost_estimate=cost or LONG,
        name=kernel.__name__,
    )(*operands)


def weights_of(chunk):
    return ((CAPS[chunk], ROWS, ROWS), BF16)


def rows_of(n):
    return ((n * D, ROWS), BF16)


def columns(n):
    return [((n * BLK * ROWS, D), BF16), ((n * BLK, CH, ROWS), BF16)]


SUM_BUF = ((SPARE + 1, SUMS, ROWS), F32)


def add_spread(chunk, list_ref, w_ref, state_ref, sum_ref, low, high):
    def four(step, _):
        for k in range(4):
            n = low + 4 * step + k
            named = list_ref[FIRST[chunk] + n]
            row = jnp.where(n < high, named >> 4, SPARE)
            sum_ref[row] += jnp.dot(state_ref[named & 15], w_ref[n], preferred_element_type=F32)
        return 0

    lax.fori_loop(0, (high - low + 3) >> 2, four, 0)


def spread_near(near_ref, list_ref, w0, w2, s0, s1, sum_ref, states):
    sum_ref[...] = jnp.zeros_like(sum_ref)
    for at, ref in enumerate((s0, s1)):
        states[at * BLK : (at + 1) * BLK] = ref[...]
    add_spread(0, near_ref, w0, states, sum_ref, 0, near_ref[TOTALS])
    add_spread(2, list_ref, w2, states, sum_ref, 0, list_ref[TOTALS + 2])


def put_coded(ref, sums, first):
    row = lax.broadcasted_iota(jnp.int32, (16, ROWS), 0)
    powers = jnp.zeros((16, ROWS), F32)
    for i in range(BLK):
        values = sums[first + i]
        largest = jnp.maximum(jnp.max(jnp.abs(values), axis=0, keepdims=True), 1e-30)
        power = jnp.ceil(jnp.log2(largest))
        coded = jnp.floor(values * (jnp.exp2(-power) * CODED) + 0.5)
        ref[i * CH : (i + 1) * CH] = coded.astype(jnp.int32).astype(jnp.int16)
        powers = jnp.where(row == i, power, powers)
    ref[BLK * CH :] = powers.astype(jnp.int32).astype(jnp.int16)


def uncoded(v):
    values = v[: BLK * CH].astype(F32).reshape(BLK, CH, ROWS)
    powers = v[BLK * CH : BLK * CH + BLK].astype(F32)
    return values * (jnp.exp2(powers) * (1.0 / CODED))[:, None, :]


def spread_far(list_ref, w3, w4, s2, s3, s4, given, far, sums, states):
    sums[...] = given[...]
    for at, ref in enumerate((s2, s3, s4)):
        states[(at + 2) * BLK : (at + 3) * BLK] = ref[...]
    for chunk, w_ref in ((3, w3), (4, w4)):
        add_spread(chunk, list_ref, w_ref, states, sums, list_ref[BEFORE + chunk], list_ref[TOTALS + chunk])
    put_coded(far, sums, 3 * BLK)


def spread_rest(near_ref, list_ref, w1, w3, w4, s2, s3, s4, given, own, back, fore, sums, states):
    sums[...] = given[...]
    for at, ref in enumerate((s2, s3, s4)):
        states[(at + 2) * BLK : (at + 3) * BLK] = ref[...]
    add_spread(1, near_ref, w1, states, sums, 0, near_ref[TOTALS + 1])
    for chunk, w_ref in ((3, w3), (4, w4)):
        add_spread(chunk, list_ref, w_ref, states, sums, 0, list_ref[BEFORE + chunk])
    own[...] = sums[:BLK]
    put_coded(back, sums, BLK)
    put_coded(fore, sums, 2 * BLK)


def spread(lists, weights, states):
    sums = ((SPARE + 1, CH, ROWS), F32)
    held = ((5 * BLK, CH, ROWS), BF16)
    part = ((BLK * CH + 16, ROWS), jnp.int16)
    w0, w1, w2, w3, w4_far, w4 = weights
    (near,) = build(spread_near, 3, [sums], [held], *lists, w0, w2, *states[:2])
    (far,) = build(spread_far, 4, [part], [sums, held], lists[1], w3, w4_far, *states[2:], near)
    near, _ = lax.optimization_barrier((near, far))
    return *build(
        spread_rest, 4, [((BLK, CH, ROWS), F32), part, part], [sums, held],
        *lists, w1, w3, w4, *states[2:], near,
    ), far


def wide_exchange(v):
    one = from_wide(v, 1)
    partner = swap_core(v)
    other = from_wide(v, -1)
    across = swap_core(one)
    return [v, partner, one, other, across]


def reduce_rows(own, back, fore, far, read=lambda v: v):
    first = lax.optimization_barrier(own + read(across_x(far)))
    return first + read(along_x(back, -1)) + read(along_x(fore, 1))


def local(embeddings, seeds, neighbours):
    code = functools.partial(coded, wide=lax.axis_index(WIDE), x=lax.axis_index("x"))
    seeds_t = jnp.swapaxes(seeds, 1, 2)
    after = lambda v, *done: lax.optimization_barrier((v, *done))[0]
    ids = split_ids(neighbours)
    two, full = prepare(embeddings, seeds_t, ids)
    one = third_turned(full, ids)
    back_two = along_x(two, 1)
    above = from_wide(full, 1)
    below = from_wide(full, -1)
    fore_one = along_x(one, -1)
    back_one = along_x(one, 1)
    back_two, fore_one, back_one, late_full, late_two = lax.optimization_barrier(
        (back_two, fore_one, back_one, full, two)
    )
    partner = swap_core(late_full)
    far_two = along_x(back_two, 1)
    fore_two = along_x(late_two, -1)
    far_one = along_x(after(fore_one, partner), -1)

    near = make_plan(
        (0, 1, 2), [code(neighbours), code(joined_ids(back_two)), code(joined_ids(fore_one))]
    )
    w0, sums, rows = build(
        build_0, 6, [weights_of(0), SUM_BUF, rows_of(9)], columns(2),
        near, two, one, back_two, back_one, fore_one, full, partner,
    )
    beside = swap_core(after(above, sums))
    w1, sums, cols, states = build(
        build_1, 4, [weights_of(1), SUM_BUF, *columns(4)], [],
        near, rows, full, partner, above, below, sums,
    )
    lists = make_plan((3,), [code(joined_ids(after(far_two, sums)))], near)
    w2, w3, sums, rows = build(
        build_2, 4, [weights_of(2), weights_of(3), SUM_BUF, rows_of(12)], [],
        lists, rows, fore_two, far_two, far_one, cols, states, sums,
    )
    part = ((BLK, SUMS, ROWS), F32)
    scratch = [SUM_BUF, ((BLK, CH, ROWS), BF16)]
    w4_far, far = build(build_far, 4, [weights_of(4), part], scratch, lists, rows, beside, sums)
    w4, own, back, fore = build(
        build_rest, 4, [weights_of(4)] + [part] * (NX - 1), scratch,
        lists, rows, beside, after(sums, far),
    )
    lists = [near, lists]
    weights = [w0, w1, w2, w3, w4_far, w4]

    total = reduce_rows(own, back, fore, far)
    scale = ALPHA / jnp.sum(total[:, CH:], axis=1, keepdims=True)
    prior = (1.0 - ALPHA) * seeds_t
    scores = total[:, :CH] * scale + prior
    for _ in range(ITERS - 1):
        states = wide_exchange(scores.astype(BF16))
        total = reduce_rows(*spread(lists, weights, states), uncoded)
        scores = total * scale + prior
    return jnp.swapaxes(scores, 1, 2)


def solution(mesh):
    fine = Mesh(mesh.devices.reshape(4, 4, 2, 4), ("z", "y", "c", "x"))
    everywhere = ("z", "y", "c", "x")
    return jax.shard_map(
        local,
        mesh=fine,
        in_specs=(P(everywhere, None, None), P(everywhere, None, None), P(everywhere, None)),
        out_specs=P(everywhere, None, None),
        check_vma=False,
    )
```

```python
import functools
import math

import jax
import jax.numpy as jnp
from jax import lax
from jax.experimental import pallas as pl
from jax.experimental.pallas import tpu as pltpu
from jax.sharding import Mesh, PartitionSpec as P

NBR = 32
ITERS = 3
SHARP = 24.0
ALPHA = 0.8
EPS = 1e-06
ROWS = 256
D = 768
CH = 64
BLK = 3
NX = 4
NW = 32
SCALE = SHARP * math.log2(math.e)
WIDE = ("z", "y", "c")
VM = pl.BlockSpec(memory_space=pltpu.VMEM)
SM = pl.BlockSpec(memory_space=pltpu.SMEM)
F32 = jnp.float32
BF16 = jnp.bfloat16
FIRST = (0, 48, 96, 144, 192)
CAPS = (44, 44, 36, 36, 40)
BASE = (0, 6, 0, 6, 12)
CHUNKS = 5
SOON = (0, 1, 2, 3, 4, 5, 8)
TOTALS = 245
BEFORE = 250
LISTS = 256
STEP = 9
CODED = 32000.0
SPARE = NX * BLK
SUMS = CH + 8
IDS = 16
CHEAP = pl.CostEstimate(flops=1000, bytes_accessed=1000, transcendentals=0)
LONG = pl.CostEstimate(flops=30_000_000_000, bytes_accessed=1000, transcendentals=0)


def along_x(v, sign):
    pairs = []
    for core in range(2):
        by = sign if core == 0 else -sign
        pairs += [(core * NX + x, core * NX + (x + by) % NX) for x in range(NX)]
    return lax.ppermute(v, ("c", "x"), pairs)


def across_x(v):
    return lax.ppermute(v, "x", [(x, (x + 2) % NX) for x in range(NX)])


def from_wide(v, sign):
    return lax.ppermute(
        v, WIDE, [((i + (2 * sign if i % 2 == 0 else -2 * sign)) % NW, i) for i in range(NW)]
    )


def swap_core(v):
    return lax.ppermute(v, "c", [(0, 1), (1, 0)])


def prep_kernel(emb_hbm, seed_hbm, ids_ref, two_ref, full_ref, emb_buf, seed_buf, sems):
    copies = [pltpu.make_async_copy(emb_hbm.at[b], emb_buf.at[b], sems.at[b]) for b in range(BLK)]
    copies.append(pltpu.make_async_copy(seed_hbm, seed_buf, sems.at[BLK]))
    for copy in copies:
        copy.start()
    for block in range(BLK):
        copies[block].wait()
        values = emb_buf[block].astype(F32)
        total = jnp.sum(values * values, axis=-1, keepdims=True)
        unit = (values * lax.rsqrt(total + EPS)).astype(BF16)
        full_ref[block * ROWS : (block + 1) * ROWS] = unit
        if block < 2:
            two_ref[block * D : (block + 1) * D] = jnp.transpose(unit)
    two_ref[2 * D :] = ids_ref[...]
    copies[BLK].wait()
    for block in range(BLK):
        full_ref[BLK * ROWS :, block * ROWS : (block + 1) * ROWS] = seed_buf[block].astype(BF16)


def prepare(embeddings, seeds_t, ids):
    far = pl.BlockSpec(memory_space=pltpu.HBM)
    return pl.pallas_call(
        prep_kernel,
        out_shape=(
            jax.ShapeDtypeStruct((2 * D + IDS, ROWS), BF16),
            jax.ShapeDtypeStruct((BLK * ROWS + CH, D), BF16),
        ),
        in_specs=[far, far, VM],
        out_specs=(VM, VM),
        scratch_shapes=[
            pltpu.VMEM((BLK, ROWS, D), BF16),
            pltpu.VMEM((BLK, CH, ROWS), F32),
            pltpu.SemaphoreType.DMA((BLK + 1,)),
        ],
        compiler_params=pltpu.CompilerParams(vmem_limit_bytes=8 << 20),
        cost_estimate=CHEAP,
        name="prep",
    )(
        pltpu.with_memory_space_constraint(embeddings, pltpu.HBM),
        pltpu.with_memory_space_constraint(seeds_t, pltpu.HBM),
        ids,
    )


def third_kernel(full_ref, ids_ref, one_ref):
    one_ref[:D] = jnp.transpose(full_ref[2 * ROWS : BLK * ROWS])
    one_ref[D:] = ids_ref[...]


def third_turned(full, ids):
    return pl.pallas_call(
        third_kernel,
        out_shape=jax.ShapeDtypeStruct((D + IDS, ROWS), BF16),
        in_specs=[VM, VM],
        out_specs=VM,
        compiler_params=pltpu.CompilerParams(vmem_limit_bytes=2 << 20),
        cost_estimate=LONG,
        name="third",
    )(full, ids)


def split_ids(neighbours):
    shown = neighbours + 1
    parts = jnp.concatenate([shown >> 4, shown & 15], axis=1).astype(BF16)
    return jnp.pad(parts, ((0, IDS - BLK), (0, ROWS - 2 * NBR)))


def joined_ids(rows):
    parts = rows[-IDS:][:BLK].astype(jnp.int32)
    return parts[:, :NBR] * 16 + parts[:, NBR : 2 * NBR] - 1


def coded(ids, wide, x):
    core = wide & 1
    device = ids // BLK
    step = (device // NX - wide + 2) & (NW - 1)
    first = 4 - 4 * core
    source = jnp.where(
        step == 2,
        0,
        jnp.where(step == 3 - 2 * core, 1, jnp.where(step == first, 2, jnp.where(step == 4 - first, 3, 4))),
    )
    adds = jnp.where(source < 2, 1, jnp.where(source < 4, 1 << STEP, 1 << (2 * STEP)))
    hit = (ids >= 0) & (device % NX == x)
    return jnp.where(hit, source * BLK + ids % BLK + 16 * adds, 0)


def plan_kernel(groups, *refs):
    code_refs = refs[: len(groups)]
    old_ref, list_ref = (refs[-2], refs[-1]) if len(refs) > len(groups) + 1 else (None, refs[-1])
    counts = [jnp.int32(0)] * CHUNKS
    if old_ref is not None:

        def copy(k, _):
            list_ref[k] = old_ref[k]
            return 0

        counts = [old_ref[TOTALS + c] for c in range(CHUNKS)]
        for c in range(2, CHUNKS):
            lax.fori_loop(FIRST[c], FIRST[c] + counts[c], copy, 0)
    for c in range(CHUNKS):
        list_ref[BEFORE + c] = counts[c]
    for ref, group in zip(code_refs, groups):
        for i in range(BLK):
            row = group * BLK + i
            chunks = (0, 1, 4) if row in SOON else (2, 3, 4)

            def body(k, packed, ref=ref, i=i, row=row, chunks=chunks):
                value = ref[i, k]
                entry = row * 16 + (value & 15)
                list_ref[FIRST[chunks[0]] + (packed & ((1 << STEP) - 1))] = entry
                list_ref[FIRST[chunks[1]] + ((packed >> STEP) & ((1 << STEP) - 1))] = entry
                list_ref[FIRST[chunks[2]] + (packed >> (2 * STEP))] = entry
                return packed + (value >> 4)

            packed = sum(counts[c] << (at * STEP) for at, c in enumerate(chunks))
            packed = lax.fori_loop(0, NBR, body, packed, unroll=8)
            for at, c in enumerate(chunks):
                counts[c] = (packed >> (at * STEP)) & ((1 << STEP) - 1)
    for c in range(CHUNKS):
        for pad in range(4):
            list_ref[FIRST[c] + counts[c] + pad] = SPARE * 16 + BASE[c]
        list_ref[TOTALS + c] = counts[c]


def make_plan(groups, codes, old=None):
    operands = [*codes] + ([old] if old is not None else [])
    return pl.pallas_call(
        functools.partial(plan_kernel, groups),
        out_shape=jax.ShapeDtypeStruct((LISTS,), jnp.int32),
        in_specs=[SM] * len(operands),
        out_specs=SM,
        compiler_params=pltpu.CompilerParams(vmem_limit_bytes=1 << 20),
        cost_estimate=LONG,
        name="plan",
    )(*operands)


def tiles(chunk, list_ref, row_ref, col_ref, state_ref, w_ref, sum_ref, low=0, high=None, base=0):
    high = list_ref[TOTALS + chunk] if high is None else high
    steps = (high - low + 3) >> 2

    def spread_four(step, live):
        for k in range(4):
            n = low + 4 * step + k
            named = list_ref[FIRST[chunk] + n]
            row = jnp.where(live & (n < high), named >> 4, SPARE)
            sum_ref[row, :CH] += jnp.dot(
                state_ref[(named & 15) - base], w_ref[n], preferred_element_type=F32
            )

    def four_tiles(step, _):
        spread_four(jnp.maximum(step - 1, 0), step > 0)
        for k in range(4):
            n = low + 4 * step + k
            named = list_ref[FIRST[chunk] + n]
            row, col = jnp.where(n < high, named >> 4, SPARE), (named & 15) - base
            place = jnp.where(row == SPARE, 0, row) * D
            cosine = jnp.dot(
                col_ref[pl.ds(pl.multiple_of(col * ROWS, ROWS), ROWS), :],
                row_ref[pl.ds(pl.multiple_of(place, D), D), :],
                preferred_element_type=F32,
            )
            weight = jnp.exp2(cosine * SCALE)
            w_ref[n] = weight.astype(BF16)
            sum_ref[row, CH:] += jnp.sum(weight.reshape(ROWS // 8, 8, ROWS), axis=0)
        return 0

    lax.fori_loop(0, steps, four_tiles, 0)
    spread_four(jnp.maximum(steps - 1, 0), steps > 0)


def put_rows(buf, refs, places):
    for ref, (at, n) in zip(refs, places):
        buf[at * D : (at + n) * D] = ref[: n * D]


def put_cols(buf, states, refs):
    for at, ref in enumerate(refs):
        buf[at * BLK * ROWS : (at + 1) * BLK * ROWS] = ref[: BLK * ROWS]
        for j in range(BLK):
            states[at * BLK + j] = ref[BLK * ROWS :, j * ROWS : (j + 1) * ROWS]


def build_0(list_ref, r0, r1, r2, r3, r4, c0, c1, w_ref, sum_ref, rows, cols, states):
    put_rows(rows, (r0, r1, r2, r3, r4), ((0, 2), (2, 1), (3, 2), (5, 1), (8, 1)))
    put_cols(cols, states, (c0, c1))
    sum_ref[...] = jnp.zeros_like(sum_ref)
    tiles(0, list_ref, rows, cols, states, w_ref, sum_ref)


def build_1(list_ref, rows, c0, c1, c2, c3, given, w_ref, sum_ref, cols, states):
    put_cols(cols, states, (c0, c1, c2, c3))
    sum_ref[...] = given[...]
    tiles(1, list_ref, rows, cols, states, w_ref, sum_ref)


def build_2(list_ref, old_rows, r0, r1, r2, cols, states, given, w2_ref, w3_ref, sum_ref, rows):
    rows[: 6 * D] = old_rows[: 6 * D]
    rows[8 * D : 9 * D] = old_rows[8 * D :]
    put_rows(rows, (r0, r1, r2), ((6, 2), (9, 2), (11, 1)))
    sum_ref[...] = given[...]
    tiles(2, list_ref, rows, cols, states, w2_ref, sum_ref)
    tiles(3, list_ref, rows, cols, states, w3_ref, sum_ref)


def power_of(values):
    return jnp.ceil(jnp.log2(jnp.maximum(values, 1e-30)))


def put_coded(ref, sums, first, degrees=False):
    row = lax.broadcasted_iota(jnp.int32, (16, ROWS), 0)
    extra = jnp.zeros((16, ROWS), F32)
    for i in range(BLK):
        values = sums[first + i, :CH]
        power = power_of(jnp.max(jnp.abs(values), axis=0, keepdims=True))
        coded = jnp.floor(values * (jnp.exp2(-power) * CODED) + 0.5)
        ref[i * CH : (i + 1) * CH] = coded.astype(jnp.int32).astype(jnp.int16)
        extra = jnp.where(row == i, power, extra)
        if degrees:
            degree = jnp.sum(sums[first + i, CH:], axis=0, keepdims=True)
            power = power_of(degree)
            scaled = degree * (jnp.exp2(-power) * CODED)
            high = jnp.floor(scaled + 0.5)
            low = jnp.floor((scaled - high) * CODED + 0.5)
            for at, part in enumerate((power, high, low)):
                extra = jnp.where(row == (at + 1) * BLK + i, part, extra)
    ref[BLK * CH :] = extra.astype(jnp.int32).astype(jnp.int16)


def uncoded(v):
    values = v[: BLK * CH].astype(F32).reshape(BLK, CH, ROWS)
    powers = v[BLK * CH : BLK * CH + BLK].astype(F32)
    return values * (jnp.exp2(powers) * (1.0 / CODED))[:, None, :]


def uncoded_degrees(v):
    power, high, low = (
        v[BLK * CH + at * BLK : BLK * CH + (at + 1) * BLK].astype(F32) for at in (1, 2, 3)
    )
    return (high + low * (1.0 / CODED)) * (jnp.exp2(power) * (1.0 / CODED))


def last_columns(list_ref, rows, c4, given, w_ref, outs, sums, states, first, low, high):
    sums[...] = given[...]
    for j in range(BLK):
        states[j] = c4[BLK * ROWS :, j * ROWS : (j + 1) * ROWS]
    tiles(4, list_ref, rows, c4, states, w_ref, sums, low, high, BASE[4])
    for at, ref in enumerate(outs):
        if first + at:
            put_coded(ref, sums, (first + at) * BLK, degrees=True)
        else:
            ref[...] = sums[:BLK]


def build_far(list_ref, rows, c4, given, w_ref, far, sums, states):
    last_columns(
        list_ref, rows, c4, given, w_ref, (far,), sums, states, 3, list_ref[BEFORE + 4], list_ref[TOTALS + 4]
    )


def build_rest(list_ref, rows, c4, given, w_ref, own, back, fore, sums, states):
    last_columns(
        list_ref, rows, c4, given, w_ref, (own, back, fore), sums, states, 0, 0, list_ref[BEFORE + 4]
    )


def build(kernel, room, outs, scratch, *operands, cost=None):
    return pl.pallas_call(
        kernel,
        out_shape=[jax.ShapeDtypeStruct(*o) for o in outs],
        in_specs=[SM if o.dtype == jnp.int32 else VM for o in operands],
        out_specs=[VM] * len(outs),
        scratch_shapes=[pltpu.VMEM(*s) for s in scratch],
        compiler_params=pltpu.CompilerParams(vmem_limit_bytes=room << 20),
        cost_estimate=cost or LONG,
        name=kernel.__name__,
    )(*operands)


def weights_of(chunk):
    return ((CAPS[chunk], ROWS, ROWS), BF16)


def rows_of(n):
    return ((n * D, ROWS), BF16)


def columns(n):
    return [((n * BLK * ROWS, D), BF16), ((n * BLK, CH, ROWS), BF16)]


SUM_BUF = ((SPARE + 1, SUMS, ROWS), F32)


def add_spread(chunk, list_ref, w_ref, state_ref, sum_ref, low, high):
    def four(step, _):
        for k in range(4):
            n = low + 4 * step + k
            named = list_ref[FIRST[chunk] + n]
            row = jnp.where(n < high, named >> 4, SPARE)
            sum_ref[row] += jnp.dot(state_ref[named & 15], w_ref[n], preferred_element_type=F32)
        return 0

    lax.fori_loop(0, (high - low + 3) >> 2, four, 0)


def spread_near(near_ref, list_ref, w0, w2, s0, s1, sum_ref, states):
    sum_ref[...] = jnp.zeros_like(sum_ref)
    for at, ref in enumerate((s0, s1)):
        states[at * BLK : (at + 1) * BLK] = ref[...]
    add_spread(0, near_ref, w0, states, sum_ref, 0, near_ref[TOTALS])
    add_spread(2, list_ref, w2, states, sum_ref, 0, list_ref[TOTALS + 2])


def spread_far(list_ref, w3, w4, s2, s3, s4, given, far, sums, states):
    sums[...] = given[...]
    for at, ref in enumerate((s2, s3, s4)):
        states[(at + 2) * BLK : (at + 3) * BLK] = ref[...]
    for chunk, w_ref in ((3, w3), (4, w4)):
        add_spread(chunk, list_ref, w_ref, states, sums, list_ref[BEFORE + chunk], list_ref[TOTALS + chunk])
    put_coded(far, sums, 3 * BLK)


def spread_rest(near_ref, list_ref, w1, w3, w4, s2, s3, s4, given, own, back, fore, sums, states):
    sums[...] = given[...]
    for at, ref in enumerate((s2, s3, s4)):
        states[(at + 2) * BLK : (at + 3) * BLK] = ref[...]
    add_spread(1, near_ref, w1, states, sums, 0, near_ref[TOTALS + 1])
    for chunk, w_ref in ((3, w3), (4, w4)):
        add_spread(chunk, list_ref, w_ref, states, sums, 0, list_ref[BEFORE + chunk])
    own[...] = sums[:BLK]
    put_coded(back, sums, BLK)
    put_coded(fore, sums, 2 * BLK)


def spread(lists, weights, states):
    sums = ((SPARE + 1, CH, ROWS), F32)
    held = ((5 * BLK, CH, ROWS), BF16)
    part = ((BLK * CH + 16, ROWS), jnp.int16)
    w0, w1, w2, w3, w4_far, w4 = weights
    (near,) = build(spread_near, 3, [sums], [held], *lists, w0, w2, *states[:2])
    (far,) = build(spread_far, 4, [part], [sums, held], lists[1], w3, w4_far, *states[2:], near)
    near, _ = lax.optimization_barrier((near, far))
    return *build(
        spread_rest, 4, [((BLK, CH, ROWS), F32), part, part], [sums, held],
        *lists, w1, w3, w4, *states[2:], near,
    ), far


def wide_exchange(v):
    one = from_wide(v, 1)
    partner = swap_core(v)
    other = from_wide(v, -1)
    across = swap_core(one)
    return [v, partner, one, other, across]


def exchange_rows(back, fore, far):
    return across_x(far), along_x(back, -1), along_x(fore, 1)


def add_rows(own, parts):
    first = lax.optimization_barrier(own + uncoded(parts[0]))
    return first + uncoded(parts[1]) + uncoded(parts[2])


def local(embeddings, seeds, neighbours):
    code = functools.partial(coded, wide=lax.axis_index(WIDE), x=lax.axis_index("x"))
    seeds_t = jnp.swapaxes(seeds, 1, 2)
    after = lambda v, *done: lax.optimization_barrier((v, *done))[0]
    ids = split_ids(neighbours)
    two, full = prepare(embeddings, seeds_t, ids)
    one = third_turned(full, ids)
    back_two = along_x(two, 1)
    above = from_wide(full, 1)
    below = from_wide(full, -1)
    fore_one = along_x(one, -1)
    back_one = along_x(one, 1)
    back_two, fore_one, back_one, late_full, late_two = lax.optimization_barrier(
        (back_two, fore_one, back_one, full, two)
    )
    partner = swap_core(late_full)
    far_two = along_x(back_two, 1)
    fore_two = along_x(late_two, -1)
    far_one = along_x(after(fore_one, partner), -1)

    near = make_plan(
        (0, 1, 2), [code(neighbours), code(joined_ids(back_two)), code(joined_ids(fore_one))]
    )
    w0, sums, rows = build(
        build_0, 6, [weights_of(0), SUM_BUF, rows_of(9)], columns(2),
        near, two, one, back_two, back_one, fore_one, full, partner,
    )
    beside = swap_core(after(above, sums))
    w1, sums, cols, states = build(
        build_1, 4, [weights_of(1), SUM_BUF, *columns(4)], [],
        near, rows, full, partner, above, below, sums,
    )
    lists = make_plan((3,), [code(joined_ids(after(far_two, sums)))], near)
    w2, w3, sums, rows = build(
        build_2, 4, [weights_of(2), weights_of(3), SUM_BUF, rows_of(12)], [],
        lists, rows, fore_two, far_two, far_one, cols, states, sums,
    )
    part = ((BLK * CH + 16, ROWS), jnp.int16)
    scratch = [SUM_BUF, ((BLK, CH, ROWS), BF16)]
    w4_far, far = build(build_far, 4, [weights_of(4), part], scratch, lists, rows, beside, sums)
    w4, own, back, fore = build(
        build_rest, 4, [weights_of(4), ((BLK, SUMS, ROWS), F32), part, part], scratch,
        lists, rows, beside, after(sums, far),
    )
    lists = [near, lists]
    weights = [w0, w1, w2, w3, w4_far, w4]

    parts = exchange_rows(back, fore, far)
    degree = jnp.sum(own[:, CH:], axis=1) + sum(uncoded_degrees(p) for p in parts)
    scale = (ALPHA / degree)[:, None, :]
    prior = (1.0 - ALPHA) * seeds_t
    scores = add_rows(own[:, :CH], parts) * scale + prior
    for _ in range(ITERS - 1):
        states = wide_exchange(scores.astype(BF16))
        own, *parts = spread(lists, weights, states)
        scores = add_rows(own, exchange_rows(*parts)) * scale + prior
    return jnp.swapaxes(scores, 1, 2)


def solution(mesh):
    fine = Mesh(mesh.devices.reshape(4, 4, 2, 4), ("z", "y", "c", "x"))
    everywhere = ("z", "y", "c", "x")
    return jax.shard_map(
        local,
        mesh=fine,
        in_specs=(P(everywhere, None, None), P(everywhere, None, None), P(everywhere, None)),
        out_specs=P(everywhere, None, None),
        check_vma=False,
    )
```

```python
import functools
import math

import jax
import jax.numpy as jnp
from jax import lax
from jax.experimental import pallas as pl
from jax.experimental.pallas import tpu as pltpu
from jax.sharding import Mesh, PartitionSpec as P

NBR = 32
ITERS = 3
SHARP = 24.0
ALPHA = 0.8
EPS = 1e-06
ROWS = 256
D = 768
CH = 64
BLK = 3
NX = 4
NW = 32
SCALE = SHARP * math.log2(math.e)
WIDE = ("z", "y", "c")
VM = pl.BlockSpec(memory_space=pltpu.VMEM)
SM = pl.BlockSpec(memory_space=pltpu.SMEM)
F32 = jnp.float32
BF16 = jnp.bfloat16
FIRST = (0, 48, 96, 144, 192)
CAPS = (44, 44, 36, 36, 40)
BASE = (0, 6, 0, 6, 12)
CHUNKS = 5
SOON = (0, 1, 2, 3, 4, 5, 8)
TOTALS = 245
BEFORE = 250
LISTS = 256
STEP = 9
CODED = 32000.0
SPARE = NX * BLK
SUMS = CH + 8
IDS = 16
CHEAP = pl.CostEstimate(flops=1000, bytes_accessed=1000, transcendentals=0)
LONG = pl.CostEstimate(flops=30_000_000_000, bytes_accessed=1000, transcendentals=0)


def along_x(v, sign):
    pairs = []
    for core in range(2):
        by = sign if core == 0 else -sign
        pairs += [(core * NX + x, core * NX + (x + by) % NX) for x in range(NX)]
    return lax.ppermute(v, ("c", "x"), pairs)


def across_x(v):
    return lax.ppermute(v, "x", [(x, (x + 2) % NX) for x in range(NX)])


def from_wide(v, sign):
    return lax.ppermute(
        v, WIDE, [((i + (2 * sign if i % 2 == 0 else -2 * sign)) % NW, i) for i in range(NW)]
    )


def swap_core(v):
    return lax.ppermute(v, "c", [(0, 1), (1, 0)])


def prep_kernel(emb_hbm, seed_hbm, ids_ref, two_ref, full_ref, emb_buf, seed_buf, sems):
    copies = [pltpu.make_async_copy(emb_hbm.at[b], emb_buf.at[b], sems.at[b]) for b in range(BLK)]
    copies.append(pltpu.make_async_copy(seed_hbm, seed_buf, sems.at[BLK]))
    for copy in copies:
        copy.start()
    for block in range(BLK):
        copies[block].wait()
        values = emb_buf[block].astype(F32)
        total = jnp.sum(values * values, axis=-1, keepdims=True)
        unit = (values * lax.rsqrt(total + EPS)).astype(BF16)
        full_ref[block * ROWS : (block + 1) * ROWS] = unit
        if block < 2:
            two_ref[block * D : (block + 1) * D] = jnp.transpose(unit)
    two_ref[2 * D :] = ids_ref[...]
    copies[BLK].wait()
    for block in range(BLK):
        full_ref[BLK * ROWS :, block * ROWS : (block + 1) * ROWS] = seed_buf[block].astype(BF16)


def prepare(embeddings, seeds_t, ids):
    far = pl.BlockSpec(memory_space=pltpu.HBM)
    return pl.pallas_call(
        prep_kernel,
        out_shape=(
            jax.ShapeDtypeStruct((2 * D + IDS, ROWS), BF16),
            jax.ShapeDtypeStruct((BLK * ROWS + CH, D), BF16),
        ),
        in_specs=[far, far, VM],
        out_specs=(VM, VM),
        scratch_shapes=[
            pltpu.VMEM((BLK, ROWS, D), BF16),
            pltpu.VMEM((BLK, CH, ROWS), F32),
            pltpu.SemaphoreType.DMA((BLK + 1,)),
        ],
        compiler_params=pltpu.CompilerParams(vmem_limit_bytes=8 << 20),
        cost_estimate=CHEAP,
        name="prep",
    )(
        pltpu.with_memory_space_constraint(embeddings, pltpu.HBM),
        pltpu.with_memory_space_constraint(seeds_t, pltpu.HBM),
        ids,
    )


def third_kernel(full_ref, ids_ref, one_ref):
    one_ref[:D] = jnp.transpose(full_ref[2 * ROWS : BLK * ROWS])
    one_ref[D:] = ids_ref[...]


def third_turned(full, ids):
    return pl.pallas_call(
        third_kernel,
        out_shape=jax.ShapeDtypeStruct((D + IDS, ROWS), BF16),
        in_specs=[VM, VM],
        out_specs=VM,
        compiler_params=pltpu.CompilerParams(vmem_limit_bytes=2 << 20),
        cost_estimate=LONG,
        name="third",
    )(full, ids)


def split_ids(neighbours):
    shown = neighbours + 1
    parts = jnp.concatenate([shown >> 4, shown & 15], axis=1).astype(BF16)
    return jnp.pad(parts, ((0, IDS - BLK), (0, ROWS - 2 * NBR)))


def joined_ids(rows):
    parts = rows[-IDS:][:BLK].astype(jnp.int32)
    return parts[:, :NBR] * 16 + parts[:, NBR : 2 * NBR] - 1


def coded(ids, wide, x):
    core = wide & 1
    device = ids // BLK
    step = (device // NX - wide + 2) & (NW - 1)
    first = 4 - 4 * core
    source = jnp.where(
        step == 2,
        0,
        jnp.where(step == 3 - 2 * core, 1, jnp.where(step == first, 2, jnp.where(step == 4 - first, 3, 4))),
    )
    adds = jnp.where(source < 2, 1, jnp.where(source < 4, 1 << STEP, 1 << (2 * STEP)))
    hit = (ids >= 0) & (device % NX == x)
    return jnp.where(hit, source * BLK + ids % BLK + 16 * adds, 0)


def plan_kernel(groups, *refs):
    code_refs = refs[: len(groups)]
    old_ref, list_ref = (refs[-2], refs[-1]) if len(refs) > len(groups) + 1 else (None, refs[-1])
    counts = [jnp.int32(0)] * CHUNKS
    if old_ref is not None:

        def copy(k, _):
            list_ref[k] = old_ref[k]
            return 0

        counts = [old_ref[TOTALS + c] for c in range(CHUNKS)]
        for c in range(2, CHUNKS):
            lax.fori_loop(FIRST[c], FIRST[c] + counts[c], copy, 0)
    for c in range(CHUNKS):
        list_ref[BEFORE + c] = counts[c]
    for ref, group in zip(code_refs, groups):
        for i in range(BLK):
            row = group * BLK + i
            chunks = (0, 1, 4) if row in SOON else (2, 3, 4)

            def body(k, packed, ref=ref, i=i, row=row, chunks=chunks):
                value = ref[i, k]
                entry = row * 16 + (value & 15)
                list_ref[FIRST[chunks[0]] + (packed & ((1 << STEP) - 1))] = entry
                list_ref[FIRST[chunks[1]] + ((packed >> STEP) & ((1 << STEP) - 1))] = entry
                list_ref[FIRST[chunks[2]] + (packed >> (2 * STEP))] = entry
                return packed + (value >> 4)

            packed = sum(counts[c] << (at * STEP) for at, c in enumerate(chunks))
            packed = lax.fori_loop(0, NBR, body, packed, unroll=8)
            for at, c in enumerate(chunks):
                counts[c] = (packed >> (at * STEP)) & ((1 << STEP) - 1)
    for c in range(CHUNKS):
        for pad in range(4):
            list_ref[FIRST[c] + counts[c] + pad] = SPARE * 16 + BASE[c]
        list_ref[TOTALS + c] = counts[c]


def make_plan(groups, codes, old=None):
    operands = [*codes] + ([old] if old is not None else [])
    return pl.pallas_call(
        functools.partial(plan_kernel, groups),
        out_shape=jax.ShapeDtypeStruct((LISTS,), jnp.int32),
        in_specs=[SM] * len(operands),
        out_specs=SM,
        compiler_params=pltpu.CompilerParams(vmem_limit_bytes=1 << 20),
        cost_estimate=LONG,
        name="plan",
    )(*operands)


def tiles(chunk, list_ref, row_ref, col_ref, state_ref, w_ref, sum_ref, low=0, high=None, base=0):
    high = list_ref[TOTALS + chunk] if high is None else high
    steps = (high - low + 3) >> 2

    def spread_four(step, live):
        for k in range(4):
            n = low + 4 * step + k
            named = list_ref[FIRST[chunk] + n]
            row = jnp.where(live & (n < high), named >> 4, SPARE)
            sum_ref[row, :CH] += jnp.dot(
                state_ref[(named & 15) - base], w_ref[n], preferred_element_type=F32
            )

    def four_tiles(step, _):
        spread_four(jnp.maximum(step - 1, 0), step > 0)
        for k in range(4):
            n = low + 4 * step + k
            named = list_ref[FIRST[chunk] + n]
            row, col = jnp.where(n < high, named >> 4, SPARE), (named & 15) - base
            place = jnp.where(row == SPARE, 0, row) * D
            cosine = jnp.dot(
                col_ref[pl.ds(pl.multiple_of(col * ROWS, ROWS), ROWS), :],
                row_ref[pl.ds(pl.multiple_of(place, D), D), :],
                preferred_element_type=F32,
            )
            weight = jnp.exp2(cosine * SCALE)
            w_ref[n] = weight.astype(BF16)
            sum_ref[row, CH:] += jnp.sum(weight.reshape(ROWS // 8, 8, ROWS), axis=0)
        return 0

    lax.fori_loop(0, steps, four_tiles, 0)
    spread_four(jnp.maximum(steps - 1, 0), steps > 0)


def put_rows(buf, refs, places):
    for ref, (at, n) in zip(refs, places):
        buf[at * D : (at + n) * D] = ref[: n * D]


def put_cols(buf, states, refs):
    for at, ref in enumerate(refs):
        buf[at * BLK * ROWS : (at + 1) * BLK * ROWS] = ref[: BLK * ROWS]
        for j in range(BLK):
            states[at * BLK + j] = ref[BLK * ROWS :, j * ROWS : (j + 1) * ROWS]


def build_0(list_ref, r0, r1, r2, r3, r4, c0, c1, w_ref, sum_ref, rows, cols, states):
    put_rows(rows, (r0, r1, r2, r3, r4), ((0, 2), (2, 1), (3, 2), (5, 1), (8, 1)))
    put_cols(cols, states, (c0, c1))
    sum_ref[...] = jnp.zeros_like(sum_ref)
    tiles(0, list_ref, rows, cols, states, w_ref, sum_ref)


def build_1(list_ref, rows, c0, c1, c2, c3, given, w_ref, sum_ref, cols, states):
    put_cols(cols, states, (c0, c1, c2, c3))
    sum_ref[...] = given[...]
    tiles(1, list_ref, rows, cols, states, w_ref, sum_ref)


def build_2(list_ref, old_rows, r0, r1, r2, cols, states, given, w2_ref, w3_ref, sum_ref, rows):
    rows[: 6 * D] = old_rows[: 6 * D]
    rows[8 * D : 9 * D] = old_rows[8 * D :]
    put_rows(rows, (r0, r1, r2), ((6, 2), (9, 2), (11, 1)))
    sum_ref[...] = given[...]
    tiles(2, list_ref, rows, cols, states, w2_ref, sum_ref)
    tiles(3, list_ref, rows, cols, states, w3_ref, sum_ref)


def power_of(values):
    return jnp.ceil(jnp.log2(jnp.maximum(values, 1e-36)))


def put_coded(ref, sums, first, degrees=False):
    row = lax.broadcasted_iota(jnp.int32, (16, ROWS), 0)
    extra = jnp.zeros((16, ROWS), F32)
    for i in range(BLK):
        values = sums[first + i, :CH]
        power = power_of(jnp.max(jnp.abs(values), axis=0, keepdims=True))
        coded = jnp.floor(values * jnp.exp2(-power) * CODED + 0.5)
        ref[i * CH : (i + 1) * CH] = coded.astype(jnp.int32).astype(jnp.int16)
        extra = jnp.where(row == i, power, extra)
        if degrees:
            degree = jnp.sum(sums[first + i, CH:], axis=0, keepdims=True)
            power = power_of(degree)
            scaled = degree * jnp.exp2(-power) * CODED
            high = jnp.floor(scaled + 0.5)
            low = jnp.floor((scaled - high) * CODED + 0.5)
            for at, part in enumerate((power, high, low)):
                extra = jnp.where(row == (at + 1) * BLK + i, part, extra)
    ref[BLK * CH :] = extra.astype(jnp.int32).astype(jnp.int16)


def uncoded(v):
    values = v[: BLK * CH].astype(F32).reshape(BLK, CH, ROWS)
    powers = v[BLK * CH : BLK * CH + BLK].astype(F32)
    return values * (1.0 / CODED) * jnp.exp2(powers)[:, None, :]


def uncoded_degrees(v):
    power, high, low = (
        v[BLK * CH + at * BLK : BLK * CH + (at + 1) * BLK].astype(F32) for at in (1, 2, 3)
    )
    return (high + low * (1.0 / CODED)) * (1.0 / CODED) * jnp.exp2(power)


def last_columns(list_ref, rows, c4, given, w_ref, outs, sums, states, first, low, high):
    sums[...] = given[...]
    for j in range(BLK):
        states[j] = c4[BLK * ROWS :, j * ROWS : (j + 1) * ROWS]
    tiles(4, list_ref, rows, c4, states, w_ref, sums, low, high, BASE[4])
    for at, ref in enumerate(outs):
        if first + at:
            put_coded(ref, sums, (first + at) * BLK, degrees=True)
        else:
            ref[...] = sums[:BLK]


def build_far(list_ref, rows, c4, given, w_ref, far, sums, states):
    last_columns(
        list_ref, rows, c4, given, w_ref, (far,), sums, states, 3, list_ref[BEFORE + 4], list_ref[TOTALS + 4]
    )


def build_rest(list_ref, rows, c4, given, w_ref, own, back, fore, sums, states):
    last_columns(
        list_ref, rows, c4, given, w_ref, (own, back, fore), sums, states, 0, 0, list_ref[BEFORE + 4]
    )


def build(kernel, room, outs, scratch, *operands, cost=None):
    return pl.pallas_call(
        kernel,
        out_shape=[jax.ShapeDtypeStruct(*o) for o in outs],
        in_specs=[SM if o.dtype == jnp.int32 else VM for o in operands],
        out_specs=[VM] * len(outs),
        scratch_shapes=[pltpu.VMEM(*s) for s in scratch],
        compiler_params=pltpu.CompilerParams(vmem_limit_bytes=room << 20),
        cost_estimate=cost or LONG,
        name=kernel.__name__,
    )(*operands)


def weights_of(chunk):
    return ((CAPS[chunk], ROWS, ROWS), BF16)


def rows_of(n):
    return ((n * D, ROWS), BF16)


def columns(n):
    return [((n * BLK * ROWS, D), BF16), ((n * BLK, CH, ROWS), BF16)]


SUM_BUF = ((SPARE + 1, SUMS, ROWS), F32)


def add_spread(chunk, list_ref, w_ref, state_ref, sum_ref, low, high):
    def four(step, _):
        for k in range(4):
            n = low + 4 * step + k
            named = list_ref[FIRST[chunk] + n]
            row = jnp.where(n < high, named >> 4, SPARE)
            sum_ref[row] += jnp.dot(state_ref[named & 15], w_ref[n], preferred_element_type=F32)
        return 0

    lax.fori_loop(0, (high - low + 3) >> 2, four, 0)


def spread_near(near_ref, list_ref, w0, w2, s0, s1, sum_ref, states):
    sum_ref[...] = jnp.zeros_like(sum_ref)
    for at, ref in enumerate((s0, s1)):
        states[at * BLK : (at + 1) * BLK] = ref[...]
    add_spread(0, near_ref, w0, states, sum_ref, 0, near_ref[TOTALS])
    add_spread(2, list_ref, w2, states, sum_ref, 0, list_ref[TOTALS + 2])


def spread_far(list_ref, w3, w4, s2, s3, s4, given, far, sums, states):
    sums[...] = given[...]
    for at, ref in enumerate((s2, s3, s4)):
        states[(at + 2) * BLK : (at + 3) * BLK] = ref[...]
    for chunk, w_ref in ((3, w3), (4, w4)):
        add_spread(chunk, list_ref, w_ref, states, sums, list_ref[BEFORE + chunk], list_ref[TOTALS + chunk])
    put_coded(far, sums, 3 * BLK)


def spread_rest(near_ref, list_ref, w1, w3, w4, s2, s3, s4, given, own, back, fore, sums, states):
    sums[...] = given[...]
    for at, ref in enumerate((s2, s3, s4)):
        states[(at + 2) * BLK : (at + 3) * BLK] = ref[...]
    add_spread(1, near_ref, w1, states, sums, 0, near_ref[TOTALS + 1])
    for chunk, w_ref in ((3, w3), (4, w4)):
        add_spread(chunk, list_ref, w_ref, states, sums, 0, list_ref[BEFORE + chunk])
    own[...] = sums[:BLK]
    put_coded(back, sums, BLK)
    put_coded(fore, sums, 2 * BLK)


def spread(lists, weights, states):
    sums = ((SPARE + 1, CH, ROWS), F32)
    held = ((5 * BLK, CH, ROWS), BF16)
    part = ((BLK * CH + 16, ROWS), jnp.int16)
    w0, w1, w2, w3, w4_far, w4 = weights
    (near,) = build(spread_near, 3, [sums], [held], *lists, w0, w2, *states[:2])
    (far,) = build(spread_far, 4, [part], [sums, held], lists[1], w3, w4_far, *states[2:], near)
    near, _ = lax.optimization_barrier((near, far))
    return *build(
        spread_rest, 4, [((BLK, CH, ROWS), F32), part, part], [sums, held],
        *lists, w1, w3, w4, *states[2:], near,
    ), far


def wide_exchange(v):
    one = from_wide(v, 1)
    partner = swap_core(v)
    other = from_wide(v, -1)
    across = swap_core(one)
    return [v, partner, one, other, across]


def exchange_rows(back, fore, far):
    return across_x(far), along_x(back, -1), along_x(fore, 1)


def add_rows(own, parts):
    first = lax.optimization_barrier(own + uncoded(parts[0]))
    return first + uncoded(parts[1]) + uncoded(parts[2])


def local(embeddings, seeds, neighbours):
    code = functools.partial(coded, wide=lax.axis_index(WIDE), x=lax.axis_index("x"))
    seeds_t = jnp.swapaxes(seeds, 1, 2)
    after = lambda v, *done: lax.optimization_barrier((v, *done))[0]
    ids = split_ids(neighbours)
    two, full = prepare(embeddings, seeds_t, ids)
    one = third_turned(full, ids)
    back_two = along_x(two, 1)
    above = from_wide(full, 1)
    below = from_wide(full, -1)
    fore_one = along_x(one, -1)
    back_one = along_x(one, 1)
    back_two, fore_one, back_one, late_full, late_two = lax.optimization_barrier(
        (back_two, fore_one, back_one, full, two)
    )
    partner = swap_core(late_full)
    far_two = along_x(back_two, 1)
    fore_two = along_x(late_two, -1)
    far_one = along_x(after(fore_one, partner), -1)

    near = make_plan(
        (0, 1, 2), [code(neighbours), code(joined_ids(back_two)), code(joined_ids(fore_one))]
    )
    w0, sums, rows = build(
        build_0, 6, [weights_of(0), SUM_BUF, rows_of(9)], columns(2),
        near, two, one, back_two, back_one, fore_one, full, partner,
    )
    beside = swap_core(after(above, sums))
    w1, sums, cols, states = build(
        build_1, 4, [weights_of(1), SUM_BUF, *columns(4)], [],
        near, rows, full, partner, above, below, sums,
    )
    lists = make_plan((3,), [code(joined_ids(after(far_two, sums)))], near)
    w2, w3, sums, rows = build(
        build_2, 4, [weights_of(2), weights_of(3), SUM_BUF, rows_of(12)], [],
        lists, rows, fore_two, far_two, far_one, cols, states, sums,
    )
    part = ((BLK * CH + 16, ROWS), jnp.int16)
    scratch = [SUM_BUF, ((BLK, CH, ROWS), BF16)]
    w4_far, far = build(build_far, 4, [weights_of(4), part], scratch, lists, rows, beside, sums)
    w4, own, back, fore = build(
        build_rest, 4, [weights_of(4), ((BLK, SUMS, ROWS), F32), part, part], scratch,
        lists, rows, beside, after(sums, far),
    )
    lists = [near, lists]
    weights = [w0, w1, w2, w3, w4_far, w4]

    parts = exchange_rows(back, fore, far)
    degree = jnp.sum(own[:, CH:], axis=1) + sum(uncoded_degrees(p) for p in parts)
    scale = (ALPHA / degree)[:, None, :]
    prior = (1.0 - ALPHA) * seeds_t
    scores = add_rows(own[:, :CH], parts) * scale + prior
    for _ in range(ITERS - 1):
        states = wide_exchange(scores.astype(BF16))
        own, *parts = spread(lists, weights, states)
        scores = add_rows(own, exchange_rows(*parts)) * scale + prior
    return jnp.swapaxes(scores, 1, 2)


def solution(mesh):
    fine = Mesh(mesh.devices.reshape(4, 4, 2, 4), ("z", "y", "c", "x"))
    everywhere = ("z", "y", "c", "x")
    return jax.shard_map(
        local,
        mesh=fine,
        in_specs=(P(everywhere, None, None), P(everywhere, None, None), P(everywhere, None)),
        out_specs=P(everywhere, None, None),
        check_vma=False,
    )
```

```python
import functools
import math

import jax
import jax.numpy as jnp
from jax import lax
from jax.experimental import pallas as pl
from jax.experimental.pallas import tpu as pltpu
from jax.sharding import Mesh, PartitionSpec as P

NBR = 32
ITERS = 3
SHARP = 24.0
ALPHA = 0.8
EPS = 1e-06
ROWS = 256
D = 768
CH = 64
BLK = 3
NX = 4
NW = 32
SCALE = SHARP * math.log2(math.e)
WIDE = ("z", "y", "c")
VM = pl.BlockSpec(memory_space=pltpu.VMEM)
SM = pl.BlockSpec(memory_space=pltpu.SMEM)
F32 = jnp.float32
BF16 = jnp.bfloat16
FIRST = (0, 48, 96, 144, 192)
CAPS = (44, 44, 36, 36, 40)
BASE = (0, 6, 0, 6, 12)
CHUNKS = 5
SOON = (0, 1, 2, 3, 4, 5, 8)
TOTALS = 245
BEFORE = 250
LISTS = 256
STEP = 9
CODED = 32000.0
SPARE = NX * BLK
SUMS = CH + 8
IDS = 16
CHEAP = pl.CostEstimate(flops=1000, bytes_accessed=1000, transcendentals=0)
LONG = pl.CostEstimate(flops=30_000_000_000, bytes_accessed=1000, transcendentals=0)


def along_x(v, sign):
    pairs = []
    for core in range(2):
        by = sign if core == 0 else -sign
        pairs += [(core * NX + x, core * NX + (x + by) % NX) for x in range(NX)]
    return lax.ppermute(v, ("c", "x"), pairs)


def across_x(v):
    return lax.ppermute(v, "x", [(x, (x + 2) % NX) for x in range(NX)])


def from_wide(v, sign):
    return lax.ppermute(
        v, WIDE, [((i + (2 * sign if i % 2 == 0 else -2 * sign)) % NW, i) for i in range(NW)]
    )


def swap_core(v):
    return lax.ppermute(v, "c", [(0, 1), (1, 0)])


def prep_kernel(emb_hbm, seed_hbm, ids_ref, two_ref, full_ref, emb_buf, seed_buf, sems):
    copies = [pltpu.make_async_copy(emb_hbm.at[b], emb_buf.at[b], sems.at[b]) for b in range(BLK)]
    copies.append(pltpu.make_async_copy(seed_hbm, seed_buf, sems.at[BLK]))
    for copy in copies:
        copy.start()
    for block in range(BLK):
        copies[block].wait()
        values = emb_buf[block].astype(F32)
        total = jnp.sum(values * values, axis=-1, keepdims=True)
        unit = (values * lax.rsqrt(total + EPS)).astype(BF16)
        full_ref[block * ROWS : (block + 1) * ROWS] = unit
        if block < 2:
            two_ref[block * D : (block + 1) * D] = jnp.transpose(unit)
    two_ref[2 * D :] = ids_ref[...]
    copies[BLK].wait()
    for block in range(BLK):
        full_ref[BLK * ROWS :, block * ROWS : (block + 1) * ROWS] = seed_buf[block].astype(BF16)


def prepare(embeddings, seeds_t, ids):
    far = pl.BlockSpec(memory_space=pltpu.HBM)
    return pl.pallas_call(
        prep_kernel,
        out_shape=(
            jax.ShapeDtypeStruct((2 * D + IDS, ROWS), BF16),
            jax.ShapeDtypeStruct((BLK * ROWS + CH, D), BF16),
        ),
        in_specs=[far, far, VM],
        out_specs=(VM, VM),
        scratch_shapes=[
            pltpu.VMEM((BLK, ROWS, D), BF16),
            pltpu.VMEM((BLK, CH, ROWS), F32),
            pltpu.SemaphoreType.DMA((BLK + 1,)),
        ],
        compiler_params=pltpu.CompilerParams(vmem_limit_bytes=8 << 20),
        cost_estimate=CHEAP,
        name="prep",
    )(
        pltpu.with_memory_space_constraint(embeddings, pltpu.HBM),
        pltpu.with_memory_space_constraint(seeds_t, pltpu.HBM),
        ids,
    )


def third_kernel(full_ref, ids_ref, one_ref):
    one_ref[:D] = jnp.transpose(full_ref[2 * ROWS : BLK * ROWS])
    one_ref[D:] = ids_ref[...]


def third_turned(full, ids):
    return pl.pallas_call(
        third_kernel,
        out_shape=jax.ShapeDtypeStruct((D + IDS, ROWS), BF16),
        in_specs=[VM, VM],
        out_specs=VM,
        compiler_params=pltpu.CompilerParams(vmem_limit_bytes=2 << 20),
        cost_estimate=LONG,
        name="third",
    )(full, ids)


def split_ids(neighbours):
    shown = neighbours + 1
    parts = jnp.concatenate([shown >> 4, shown & 15], axis=1).astype(BF16)
    return jnp.pad(parts, ((0, IDS - BLK), (0, ROWS - 2 * NBR)))


def joined_ids(rows):
    parts = rows[-IDS:][:BLK].astype(jnp.int32)
    return parts[:, :NBR] * 16 + parts[:, NBR : 2 * NBR] - 1


def coded(ids, wide, x):
    core = wide & 1
    device = ids // BLK
    step = (device // NX - wide + 2) & (NW - 1)
    first = 4 - 4 * core
    source = jnp.where(
        step == 2,
        0,
        jnp.where(step == 3 - 2 * core, 1, jnp.where(step == first, 2, jnp.where(step == 4 - first, 3, 4))),
    )
    adds = jnp.where(source < 2, 1, jnp.where(source < 4, 1 << STEP, 1 << (2 * STEP)))
    hit = (ids >= 0) & (device % NX == x)
    return jnp.where(hit, source * BLK + ids % BLK + 16 * adds, 0)


def plan_kernel(groups, *refs):
    code_refs = refs[: len(groups)]
    old_ref, list_ref = (refs[-2], refs[-1]) if len(refs) > len(groups) + 1 else (None, refs[-1])
    counts = [jnp.int32(0)] * CHUNKS
    if old_ref is not None:

        def copy(k, _):
            list_ref[k] = old_ref[k]
            return 0

        counts = [old_ref[TOTALS + c] for c in range(CHUNKS)]
        for c in range(2, CHUNKS):
            lax.fori_loop(FIRST[c], FIRST[c] + counts[c], copy, 0)
    for c in range(CHUNKS):
        list_ref[BEFORE + c] = counts[c]
    for ref, group in zip(code_refs, groups):
        for i in range(BLK):
            row = group * BLK + i
            chunks = (0, 1, 4) if row in SOON else (2, 3, 4)

            def body(k, packed, ref=ref, i=i, row=row, chunks=chunks):
                value = ref[i, k]
                entry = row * 16 + (value & 15)
                list_ref[FIRST[chunks[0]] + (packed & ((1 << STEP) - 1))] = entry
                list_ref[FIRST[chunks[1]] + ((packed >> STEP) & ((1 << STEP) - 1))] = entry
                list_ref[FIRST[chunks[2]] + (packed >> (2 * STEP))] = entry
                return packed + (value >> 4)

            packed = sum(counts[c] << (at * STEP) for at, c in enumerate(chunks))
            packed = lax.fori_loop(0, NBR, body, packed, unroll=8)
            for at, c in enumerate(chunks):
                counts[c] = (packed >> (at * STEP)) & ((1 << STEP) - 1)
    for c in range(CHUNKS):
        for pad in range(4):
            list_ref[FIRST[c] + counts[c] + pad] = SPARE * 16 + BASE[c]
        list_ref[TOTALS + c] = counts[c]


def make_plan(groups, codes, old=None):
    operands = [*codes] + ([old] if old is not None else [])
    return pl.pallas_call(
        functools.partial(plan_kernel, groups),
        out_shape=jax.ShapeDtypeStruct((LISTS,), jnp.int32),
        in_specs=[SM] * len(operands),
        out_specs=SM,
        compiler_params=pltpu.CompilerParams(vmem_limit_bytes=1 << 20),
        cost_estimate=LONG,
        name="plan",
    )(*operands)


def tiles(chunk, list_ref, row_ref, col_ref, state_ref, w_ref, sum_ref, low=0, high=None, base=0):
    high = list_ref[TOTALS + chunk] if high is None else high
    steps = (high - low + 3) >> 2

    def spread_four(step, live):
        for k in range(4):
            n = low + 4 * step + k
            named = list_ref[FIRST[chunk] + n]
            row = jnp.where(live & (n < high), named >> 4, SPARE)
            sum_ref[row, :CH] += jnp.dot(
                state_ref[(named & 15) - base], w_ref[n], preferred_element_type=F32
            )

    def four_tiles(step, _):
        spread_four(jnp.maximum(step - 1, 0), step > 0)
        for k in range(4):
            n = low + 4 * step + k
            named = list_ref[FIRST[chunk] + n]
            row, col = jnp.where(n < high, named >> 4, SPARE), (named & 15) - base
            place = jnp.where(row == SPARE, 0, row) * D
            cosine = jnp.dot(
                col_ref[pl.ds(pl.multiple_of(col * ROWS, ROWS), ROWS), :],
                row_ref[pl.ds(pl.multiple_of(place, D), D), :],
                preferred_element_type=F32,
            )
            weight = jnp.exp2(cosine * SCALE)
            w_ref[n] = weight.astype(BF16)
            sum_ref[row, CH:] += jnp.sum(weight.reshape(ROWS // 8, 8, ROWS), axis=0)
        return 0

    lax.fori_loop(0, steps, four_tiles, 0)
    spread_four(jnp.maximum(steps - 1, 0), steps > 0)


def put_rows(buf, refs, places):
    for ref, (at, n) in zip(refs, places):
        buf[at * D : (at + n) * D] = ref[: n * D]


def put_cols(buf, states, refs):
    for at, ref in enumerate(refs):
        buf[at * BLK * ROWS : (at + 1) * BLK * ROWS] = ref[: BLK * ROWS]
        for j in range(BLK):
            states[at * BLK + j] = ref[BLK * ROWS :, j * ROWS : (j + 1) * ROWS]


def build_0(list_ref, r0, r1, r2, r3, r4, c0, c1, w_ref, sum_ref, rows, cols, states):
    put_rows(rows, (r0, r1, r2, r3, r4), ((0, 2), (2, 1), (3, 2), (5, 1), (8, 1)))
    put_cols(cols, states, (c0, c1))
    sum_ref[...] = jnp.zeros_like(sum_ref)
    tiles(0, list_ref, rows, cols, states, w_ref, sum_ref)


def build_1(list_ref, rows, c0, c1, given, w_ref, sum_ref, cols, states):
    put_cols(cols, states, (c0, c1))
    sum_ref[...] = given[...]
    tiles(1, list_ref, rows, cols, states, w_ref, sum_ref, base=BASE[1])


def build_2(list_ref, old_rows, r0, r1, r2, cols, states, cols2, states2, given, w2_ref, w3_ref, sum_ref, rows):
    rows[: 6 * D] = old_rows[: 6 * D]
    rows[8 * D : 9 * D] = old_rows[8 * D :]
    put_rows(rows, (r0, r1, r2), ((6, 2), (9, 2), (11, 1)))
    sum_ref[...] = given[...]
    tiles(2, list_ref, rows, cols, states, w2_ref, sum_ref)
    tiles(3, list_ref, rows, cols2, states2, w3_ref, sum_ref, base=BASE[3])


def power_of(values):
    return jnp.ceil(jnp.log2(jnp.maximum(values, 1e-36)))


def put_coded(ref, sums, first, degrees=False):
    row = lax.broadcasted_iota(jnp.int32, (16, ROWS), 0)
    extra = jnp.zeros((16, ROWS), F32)
    for i in range(BLK):
        values = sums[first + i, :CH]
        power = power_of(jnp.max(jnp.abs(values), axis=0, keepdims=True))
        coded = jnp.floor(values * jnp.exp2(-power) * CODED + 0.5)
        ref[i * CH : (i + 1) * CH] = coded.astype(jnp.int32).astype(jnp.int16)
        extra = jnp.where(row == i, power, extra)
        if degrees:
            degree = jnp.sum(sums[first + i, CH:], axis=0, keepdims=True)
            power = power_of(degree)
            scaled = degree * jnp.exp2(-power) * CODED
            high = jnp.floor(scaled + 0.5)
            low = jnp.floor((scaled - high) * CODED + 0.5)
            for at, part in enumerate((power, high, low)):
                extra = jnp.where(row == (at + 1) * BLK + i, part, extra)
    ref[BLK * CH :] = extra.astype(jnp.int32).astype(jnp.int16)


def uncoded(v):
    values = v[: BLK * CH].astype(F32).reshape(BLK, CH, ROWS)
    powers = v[BLK * CH : BLK * CH + BLK].astype(F32)
    return values * (1.0 / CODED) * jnp.exp2(powers)[:, None, :]


def uncoded_degrees(v):
    power, high, low = (
        v[BLK * CH + at * BLK : BLK * CH + (at + 1) * BLK].astype(F32) for at in (1, 2, 3)
    )
    return (high + low * (1.0 / CODED)) * (1.0 / CODED) * jnp.exp2(power)


def last_columns(list_ref, rows, c4, given, w_ref, outs, sums, states, first, low, high):
    sums[...] = given[...]
    for j in range(BLK):
        states[j] = c4[BLK * ROWS :, j * ROWS : (j + 1) * ROWS]
    tiles(4, list_ref, rows, c4, states, w_ref, sums, low, high, BASE[4])
    for at, ref in enumerate(outs):
        if first + at:
            put_coded(ref, sums, (first + at) * BLK, degrees=True)
        else:
            ref[...] = sums[:BLK]


def build_far(list_ref, rows, c4, given, w_ref, far, sums, states):
    last_columns(
        list_ref, rows, c4, given, w_ref, (far,), sums, states, 3, list_ref[BEFORE + 4], list_ref[TOTALS + 4]
    )


def build_rest(list_ref, rows, c4, given, w_ref, own, back, fore, sums, states):
    last_columns(
        list_ref, rows, c4, given, w_ref, (own, back, fore), sums, states, 0, 0, list_ref[BEFORE + 4]
    )


def build(kernel, room, outs, scratch, *operands, cost=None):
    return pl.pallas_call(
        kernel,
        out_shape=[jax.ShapeDtypeStruct(*o) for o in outs],
        in_specs=[SM if o.dtype == jnp.int32 else VM for o in operands],
        out_specs=[VM] * len(outs),
        scratch_shapes=[pltpu.VMEM(*s) for s in scratch],
        compiler_params=pltpu.CompilerParams(vmem_limit_bytes=room << 20),
        cost_estimate=cost or LONG,
        name=kernel.__name__,
    )(*operands)


def weights_of(chunk):
    return ((CAPS[chunk], ROWS, ROWS), BF16)


def rows_of(n):
    return ((n * D, ROWS), BF16)


def columns(n):
    return [((n * BLK * ROWS, D), BF16), ((n * BLK, CH, ROWS), BF16)]


SUM_BUF = ((SPARE + 1, SUMS, ROWS), F32)


def add_spread(chunk, list_ref, w_ref, state_ref, sum_ref, low, high):
    def four(step, _):
        for k in range(4):
            n = low + 4 * step + k
            named = list_ref[FIRST[chunk] + n]
            row = jnp.where(n < high, named >> 4, SPARE)
            sum_ref[row] += jnp.dot(state_ref[named & 15], w_ref[n], preferred_element_type=F32)
        return 0

    lax.fori_loop(0, (high - low + 3) >> 2, four, 0)


def spread_near(near_ref, list_ref, w0, w2, s0, s1, sum_ref, states):
    sum_ref[...] = jnp.zeros_like(sum_ref)
    for at, ref in enumerate((s0, s1)):
        states[at * BLK : (at + 1) * BLK] = ref[...]
    add_spread(0, near_ref, w0, states, sum_ref, 0, near_ref[TOTALS])
    add_spread(2, list_ref, w2, states, sum_ref, 0, list_ref[TOTALS + 2])


def spread_far(list_ref, w3, w4, s2, s3, s4, given, far, sums, states):
    sums[...] = given[...]
    for at, ref in enumerate((s2, s3, s4)):
        states[(at + 2) * BLK : (at + 3) * BLK] = ref[...]
    for chunk, w_ref in ((3, w3), (4, w4)):
        add_spread(chunk, list_ref, w_ref, states, sums, list_ref[BEFORE + chunk], list_ref[TOTALS + chunk])
    put_coded(far, sums, 3 * BLK)


def spread_rest(near_ref, list_ref, w1, w3, w4, s2, s3, s4, given, own, back, fore, sums, states):
    sums[...] = given[...]
    for at, ref in enumerate((s2, s3, s4)):
        states[(at + 2) * BLK : (at + 3) * BLK] = ref[...]
    add_spread(1, near_ref, w1, states, sums, 0, near_ref[TOTALS + 1])
    for chunk, w_ref in ((3, w3), (4, w4)):
        add_spread(chunk, list_ref, w_ref, states, sums, 0, list_ref[BEFORE + chunk])
    own[...] = sums[:BLK]
    put_coded(back, sums, BLK)
    put_coded(fore, sums, 2 * BLK)


def spread(lists, weights, states):
    sums = ((SPARE + 1, CH, ROWS), F32)
    held = ((5 * BLK, CH, ROWS), BF16)
    part = ((BLK * CH + 16, ROWS), jnp.int16)
    w0, w1, w2, w3, w4_far, w4 = weights
    (near,) = build(spread_near, 3, [sums], [held], *lists, w0, w2, *states[:2])
    (far,) = build(spread_far, 4, [part], [sums, held], lists[1], w3, w4_far, *states[2:], near)
    near, _ = lax.optimization_barrier((near, far))
    return *build(
        spread_rest, 4, [((BLK, CH, ROWS), F32), part, part], [sums, held],
        *lists, w1, w3, w4, *states[2:], near,
    ), far


def wide_exchange(v):
    one = from_wide(v, 1)
    partner = swap_core(v)
    other = from_wide(v, -1)
    across = swap_core(one)
    return [v, partner, one, other, across]


def exchange_rows(back, fore, far):
    return across_x(far), along_x(back, -1), along_x(fore, 1)


def add_rows(own, parts):
    first = lax.optimization_barrier(own + uncoded(parts[0]))
    return first + uncoded(parts[1]) + uncoded(parts[2])


def local(embeddings, seeds, neighbours):
    code = functools.partial(coded, wide=lax.axis_index(WIDE), x=lax.axis_index("x"))
    seeds_t = jnp.swapaxes(seeds, 1, 2)
    after = lambda v, *done: lax.optimization_barrier((v, *done))[0]
    ids = split_ids(neighbours)
    two, full = prepare(embeddings, seeds_t, ids)
    one = third_turned(full, ids)
    back_two = along_x(two, 1)
    above = from_wide(full, 1)
    below = from_wide(full, -1)
    fore_one = along_x(one, -1)
    back_one = along_x(one, 1)
    back_two, fore_one, back_one, late_full, late_two = lax.optimization_barrier(
        (back_two, fore_one, back_one, full, two)
    )
    partner = swap_core(late_full)
    far_two = along_x(back_two, 1)
    fore_two = along_x(late_two, -1)
    far_one = along_x(after(fore_one, partner), -1)

    near = make_plan(
        (0, 1, 2), [code(neighbours), code(joined_ids(back_two)), code(joined_ids(fore_one))]
    )
    w0, sums, rows, *near_cols = build(
        build_0, 4, [weights_of(0), SUM_BUF, rows_of(9), *columns(2)], [],
        near, two, one, back_two, back_one, fore_one, full, partner,
    )
    beside = swap_core(after(above, sums))
    w1, sums, *wide_cols = build(
        build_1, 4, [weights_of(1), SUM_BUF, *columns(2)], [], near, rows, above, below, sums
    )
    lists = make_plan((3,), [code(joined_ids(after(far_two, sums)))], near)
    w2, w3, sums, rows = build(
        build_2, 4, [weights_of(2), weights_of(3), SUM_BUF, rows_of(12)], [],
        lists, rows, fore_two, far_two, far_one, *near_cols, *wide_cols, sums,
    )
    part = ((BLK * CH + 16, ROWS), jnp.int16)
    scratch = [SUM_BUF, ((BLK, CH, ROWS), BF16)]
    w4_far, far = build(build_far, 4, [weights_of(4), part], scratch, lists, rows, beside, sums)
    w4, own, back, fore = build(
        build_rest, 4, [weights_of(4), ((BLK, SUMS, ROWS), F32), part, part], scratch,
        lists, rows, beside, after(sums, far),
    )
    lists = [near, lists]
    weights = [w0, w1, w2, w3, w4_far, w4]

    parts = exchange_rows(back, fore, far)
    degree = jnp.sum(own[:, CH:], axis=1) + sum(uncoded_degrees(p) for p in parts)
    scale = (ALPHA / degree)[:, None, :]
    prior = (1.0 - ALPHA) * seeds_t
    scores = add_rows(own[:, :CH], parts) * scale + prior
    for _ in range(ITERS - 1):
        states = wide_exchange(scores.astype(BF16))
        own, *parts = spread(lists, weights, states)
        scores = add_rows(own, exchange_rows(*parts)) * scale + prior
    return jnp.swapaxes(scores, 1, 2)


def solution(mesh):
    fine = Mesh(mesh.devices.reshape(4, 4, 2, 4), ("z", "y", "c", "x"))
    everywhere = ("z", "y", "c", "x")
    return jax.shard_map(
        local,
        mesh=fine,
        in_specs=(P(everywhere, None, None), P(everywhere, None, None), P(everywhere, None)),
        out_specs=P(everywhere, None, None),
        check_vma=False,
    )
```

```python
import functools
import math

import jax
import jax.numpy as jnp
from jax import lax
from jax.experimental import pallas as pl
from jax.experimental.pallas import tpu as pltpu
from jax.sharding import Mesh, PartitionSpec as P

NBR = 32
ITERS = 3
SHARP = 24.0
ALPHA = 0.8
EPS = 1e-06
ROWS = 256
D = 768
CH = 64
BLK = 3
NX = 4
NW = 32
SCALE = SHARP * math.log2(math.e)
WIDE = ("z", "y", "c")
VM = pl.BlockSpec(memory_space=pltpu.VMEM)
SM = pl.BlockSpec(memory_space=pltpu.SMEM)
F32 = jnp.float32
BF16 = jnp.bfloat16
FIRST = (0, 48, 96, 144, 192)
CAPS = (44, 44, 36, 36, 40)
BASE = (0, 6, 0, 6, 12)
CHUNKS = 5
SOON = (0, 1, 2, 3, 4, 5, 8)
TOTALS = 245
BEFORE = 250
LISTS = 256
STEP = 9
CODED = 32000.0
SPARE = NX * BLK
SUMS = CH + 8
IDS = 16
CHEAP = pl.CostEstimate(flops=1000, bytes_accessed=1000, transcendentals=0)
LONG = pl.CostEstimate(flops=30_000_000_000, bytes_accessed=1000, transcendentals=0)


def along_x(v, sign):
    pairs = []
    for core in range(2):
        by = sign if core == 0 else -sign
        pairs += [(core * NX + x, core * NX + (x + by) % NX) for x in range(NX)]
    return lax.ppermute(v, ("c", "x"), pairs)


def across_x(v):
    return lax.ppermute(v, "x", [(x, (x + 2) % NX) for x in range(NX)])


def from_wide(v, sign):
    return lax.ppermute(
        v, WIDE, [((i + (2 * sign if i % 2 == 0 else -2 * sign)) % NW, i) for i in range(NW)]
    )


def swap_core(v):
    return lax.ppermute(v, "c", [(0, 1), (1, 0)])


def prep_kernel(emb_hbm, seed_hbm, ids_ref, two_ref, full_ref, emb_buf, seed_buf, sems):
    copies = [pltpu.make_async_copy(emb_hbm.at[b], emb_buf.at[b], sems.at[b]) for b in range(BLK)]
    copies.append(pltpu.make_async_copy(seed_hbm, seed_buf, sems.at[BLK]))
    for copy in copies:
        copy.start()
    for block in range(BLK):
        copies[block].wait()
        values = emb_buf[block].astype(F32)
        total = jnp.sum(values * values, axis=-1, keepdims=True)
        unit = (values * lax.rsqrt(total + EPS)).astype(BF16)
        full_ref[block * ROWS : (block + 1) * ROWS] = unit
        if block < 2:
            two_ref[block * D : (block + 1) * D] = jnp.transpose(unit)
    two_ref[2 * D :] = ids_ref[...]
    copies[BLK].wait()
    for block in range(BLK):
        full_ref[BLK * ROWS :, block * ROWS : (block + 1) * ROWS] = seed_buf[block].astype(BF16)


def prepare(embeddings, seeds_t, ids):
    far = pl.BlockSpec(memory_space=pltpu.HBM)
    return pl.pallas_call(
        prep_kernel,
        out_shape=(
            jax.ShapeDtypeStruct((2 * D + IDS, ROWS), BF16),
            jax.ShapeDtypeStruct((BLK * ROWS + CH, D), BF16),
        ),
        in_specs=[far, far, VM],
        out_specs=(VM, VM),
        scratch_shapes=[
            pltpu.VMEM((BLK, ROWS, D), BF16),
            pltpu.VMEM((BLK, CH, ROWS), F32),
            pltpu.SemaphoreType.DMA((BLK + 1,)),
        ],
        compiler_params=pltpu.CompilerParams(vmem_limit_bytes=8 << 20),
        cost_estimate=CHEAP,
        name="prep",
    )(
        pltpu.with_memory_space_constraint(embeddings, pltpu.HBM),
        pltpu.with_memory_space_constraint(seeds_t, pltpu.HBM),
        ids,
    )


def third_kernel(full_ref, ids_ref, one_ref):
    one_ref[:D] = jnp.transpose(full_ref[2 * ROWS : BLK * ROWS])
    one_ref[D:] = ids_ref[...]


def third_turned(full, ids):
    return pl.pallas_call(
        third_kernel,
        out_shape=jax.ShapeDtypeStruct((D + IDS, ROWS), BF16),
        in_specs=[VM, VM],
        out_specs=VM,
        compiler_params=pltpu.CompilerParams(vmem_limit_bytes=2 << 20),
        cost_estimate=LONG,
        name="third",
    )(full, ids)


def split_ids(neighbours):
    shown = neighbours + 1
    parts = jnp.concatenate([shown >> 4, shown & 15], axis=1).astype(BF16)
    return jnp.pad(parts, ((0, IDS - BLK), (0, ROWS - 2 * NBR)))


def joined_ids(rows):
    parts = rows[-IDS:][:BLK].astype(jnp.int32)
    return parts[:, :NBR] * 16 + parts[:, NBR : 2 * NBR] - 1


def coded(ids, wide, x):
    core = wide & 1
    device = ids // BLK
    step = (device // NX - wide + 2) & (NW - 1)
    first = 4 - 4 * core
    source = jnp.where(
        step == 2,
        0,
        jnp.where(step == 3 - 2 * core, 1, jnp.where(step == first, 2, jnp.where(step == 4 - first, 3, 4))),
    )
    adds = jnp.where(source < 2, 1, jnp.where(source < 4, 1 << STEP, 1 << (2 * STEP)))
    hit = (ids >= 0) & (device % NX == x)
    return jnp.where(hit, source * BLK + ids % BLK + 16 * adds, 0)


def plan_kernel(groups, *refs):
    code_refs = refs[: len(groups)]
    old_ref, list_ref = (refs[-2], refs[-1]) if len(refs) > len(groups) + 1 else (None, refs[-1])
    counts = [jnp.int32(0)] * CHUNKS
    if old_ref is not None:

        def copy(k, _):
            list_ref[k] = old_ref[k]
            return 0

        counts = [old_ref[TOTALS + c] for c in range(CHUNKS)]
        for c in range(2, CHUNKS):
            lax.fori_loop(FIRST[c], FIRST[c] + counts[c], copy, 0)
    for c in range(CHUNKS):
        list_ref[BEFORE + c] = counts[c]
    for ref, group in zip(code_refs, groups):
        for i in range(BLK):
            row = group * BLK + i
            chunks = (0, 1, 4) if row in SOON else (2, 3, 4)

            def body(k, packed, ref=ref, i=i, row=row, chunks=chunks):
                value = ref[i, k]
                entry = row * 16 + (value & 15)
                list_ref[FIRST[chunks[0]] + (packed & ((1 << STEP) - 1))] = entry
                list_ref[FIRST[chunks[1]] + ((packed >> STEP) & ((1 << STEP) - 1))] = entry
                list_ref[FIRST[chunks[2]] + (packed >> (2 * STEP))] = entry
                return packed + (value >> 4)

            packed = sum(counts[c] << (at * STEP) for at, c in enumerate(chunks))
            packed = lax.fori_loop(0, NBR, body, packed, unroll=NBR)
            for at, c in enumerate(chunks):
                counts[c] = (packed >> (at * STEP)) & ((1 << STEP) - 1)
    for c in range(CHUNKS):
        for pad in range(4):
            list_ref[FIRST[c] + counts[c] + pad] = SPARE * 16 + BASE[c]
        list_ref[TOTALS + c] = counts[c]


def make_plan(groups, codes, old=None):
    operands = [*codes] + ([old] if old is not None else [])
    return pl.pallas_call(
        functools.partial(plan_kernel, groups),
        out_shape=jax.ShapeDtypeStruct((LISTS,), jnp.int32),
        in_specs=[SM] * len(operands),
        out_specs=SM,
        compiler_params=pltpu.CompilerParams(vmem_limit_bytes=1 << 20),
        cost_estimate=LONG,
        name="plan",
    )(*operands)


def tiles(chunk, list_ref, row_ref, col_ref, state_ref, w_ref, sum_ref, low=0, high=None, base=0):
    high = list_ref[TOTALS + chunk] if high is None else high
    steps = (high - low + 3) >> 2

    def spread_four(step, live):
        for k in range(4):
            n = low + 4 * step + k
            named = list_ref[FIRST[chunk] + n]
            row = jnp.where(live & (n < high), named >> 4, SPARE)
            sum_ref[row, :CH] += jnp.dot(
                state_ref[(named & 15) - base], w_ref[n], preferred_element_type=F32
            )

    def four_tiles(step, _):
        spread_four(jnp.maximum(step - 1, 0), step > 0)
        for k in range(4):
            n = low + 4 * step + k
            named = list_ref[FIRST[chunk] + n]
            row, col = jnp.where(n < high, named >> 4, SPARE), (named & 15) - base
            place = jnp.where(row == SPARE, 0, row) * D
            cosine = jnp.dot(
                col_ref[pl.ds(pl.multiple_of(col * ROWS, ROWS), ROWS), :],
                row_ref[pl.ds(pl.multiple_of(place, D), D), :],
                preferred_element_type=F32,
            )
            weight = jnp.exp2(cosine * SCALE)
            w_ref[n] = weight.astype(BF16)
            sum_ref[row, CH:] += jnp.sum(weight.reshape(ROWS // 8, 8, ROWS), axis=0)
        return 0

    lax.fori_loop(0, steps, four_tiles, 0)
    spread_four(jnp.maximum(steps - 1, 0), steps > 0)


def put_rows(buf, refs, places):
    for ref, (at, n) in zip(refs, places):
        buf[at * D : (at + n) * D] = ref[: n * D]


def put_cols(buf, states, refs):
    for at, ref in enumerate(refs):
        buf[at * BLK * ROWS : (at + 1) * BLK * ROWS] = ref[: BLK * ROWS]
        for j in range(BLK):
            states[at * BLK + j] = ref[BLK * ROWS :, j * ROWS : (j + 1) * ROWS]


def build_0(list_ref, r0, r1, r2, r3, r4, c0, c1, w_ref, sum_ref, rows, cols, states):
    put_rows(rows, (r0, r1, r2, r3, r4), ((0, 2), (2, 1), (3, 2), (5, 1), (8, 1)))
    put_cols(cols, states, (c0, c1))
    sum_ref[...] = jnp.zeros_like(sum_ref)
    tiles(0, list_ref, rows, cols, states, w_ref, sum_ref)


def build_1(list_ref, rows, c0, c1, given, w_ref, sum_ref, cols, states):
    put_cols(cols, states, (c0, c1))
    sum_ref[...] = given[...]
    tiles(1, list_ref, rows, cols, states, w_ref, sum_ref, base=BASE[1])


def build_2(list_ref, old_rows, r0, r1, r2, cols, states, cols2, states2, given, w2_ref, w3_ref, sum_ref, rows):
    rows[: 6 * D] = old_rows[: 6 * D]
    rows[8 * D : 9 * D] = old_rows[8 * D :]
    put_rows(rows, (r0, r1, r2), ((6, 2), (9, 2), (11, 1)))
    sum_ref[...] = given[...]
    tiles(2, list_ref, rows, cols, states, w2_ref, sum_ref)
    tiles(3, list_ref, rows, cols2, states2, w3_ref, sum_ref, base=BASE[3])


def power_of(values):
    return jnp.ceil(jnp.log2(jnp.maximum(values, 1e-36)))


def put_coded(ref, sums, first, degrees=False):
    row = lax.broadcasted_iota(jnp.int32, (16, ROWS), 0)
    extra = jnp.zeros((16, ROWS), F32)
    for i in range(BLK):
        values = sums[first + i, :CH]
        power = power_of(jnp.max(jnp.abs(values), axis=0, keepdims=True))
        coded = jnp.floor(values * jnp.exp2(-power) * CODED + 0.5)
        ref[i * CH : (i + 1) * CH] = coded.astype(jnp.int32).astype(jnp.int16)
        extra = jnp.where(row == i, power, extra)
        if degrees:
            degree = jnp.sum(sums[first + i, CH:], axis=0, keepdims=True)
            power = power_of(degree)
            scaled = degree * jnp.exp2(-power) * CODED
            high = jnp.floor(scaled + 0.5)
            low = jnp.floor((scaled - high) * CODED + 0.5)
            for at, part in enumerate((power, high, low)):
                extra = jnp.where(row == (at + 1) * BLK + i, part, extra)
    ref[BLK * CH :] = extra.astype(jnp.int32).astype(jnp.int16)


def uncoded(v):
    values = v[: BLK * CH].astype(F32).reshape(BLK, CH, ROWS)
    powers = v[BLK * CH : BLK * CH + BLK].astype(F32)
    return values * (1.0 / CODED) * jnp.exp2(powers)[:, None, :]


def uncoded_degrees(v):
    power, high, low = (
        v[BLK * CH + at * BLK : BLK * CH + (at + 1) * BLK].astype(F32) for at in (1, 2, 3)
    )
    return (high + low * (1.0 / CODED)) * (1.0 / CODED) * jnp.exp2(power)


def last_columns(list_ref, rows, c4, given, w_ref, outs, sums, states, first, low, high):
    sums[...] = given[...]
    for j in range(BLK):
        states[j] = c4[BLK * ROWS :, j * ROWS : (j + 1) * ROWS]
    tiles(4, list_ref, rows, c4, states, w_ref, sums, low, high, BASE[4])
    for at, ref in enumerate(outs):
        if first + at:
            put_coded(ref, sums, (first + at) * BLK, degrees=True)
        else:
            ref[...] = sums[:BLK]


def build_far(list_ref, rows, c4, given, w_ref, far, sums, states):
    last_columns(
        list_ref, rows, c4, given, w_ref, (far,), sums, states, 3, list_ref[BEFORE + 4], list_ref[TOTALS + 4]
    )


def build_rest(list_ref, rows, c4, given, w_ref, own, back, fore, sums, states):
    last_columns(
        list_ref, rows, c4, given, w_ref, (own, back, fore), sums, states, 0, 0, list_ref[BEFORE + 4]
    )


def build(kernel, room, outs, scratch, *operands, cost=None):
    return pl.pallas_call(
        kernel,
        out_shape=[jax.ShapeDtypeStruct(*o) for o in outs],
        in_specs=[SM if o.dtype == jnp.int32 else VM for o in operands],
        out_specs=[VM] * len(outs),
        scratch_shapes=[pltpu.VMEM(*s) for s in scratch],
        compiler_params=pltpu.CompilerParams(vmem_limit_bytes=room << 20),
        cost_estimate=cost or LONG,
        name=kernel.__name__,
    )(*operands)


def weights_of(chunk):
    return ((CAPS[chunk], ROWS, ROWS), BF16)


def rows_of(n):
    return ((n * D, ROWS), BF16)


def columns(n):
    return [((n * BLK * ROWS, D), BF16), ((n * BLK, CH, ROWS), BF16)]


SUM_BUF = ((SPARE + 1, SUMS, ROWS), F32)


def add_spread(chunk, list_ref, w_ref, state_ref, sum_ref, low, high):
    def four(step, _):
        for k in range(4):
            n = low + 4 * step + k
            named = list_ref[FIRST[chunk] + n]
            row = jnp.where(n < high, named >> 4, SPARE)
            sum_ref[row] += jnp.dot(state_ref[named & 15], w_ref[n], preferred_element_type=F32)
        return 0

    lax.fori_loop(0, (high - low + 3) >> 2, four, 0)


def spread_near(near_ref, list_ref, w0, w2, s0, s1, sum_ref, states):
    sum_ref[...] = jnp.zeros_like(sum_ref)
    for at, ref in enumerate((s0, s1)):
        states[at * BLK : (at + 1) * BLK] = ref[...]
    add_spread(0, near_ref, w0, states, sum_ref, 0, near_ref[TOTALS])
    add_spread(2, list_ref, w2, states, sum_ref, 0, list_ref[TOTALS + 2])


def spread_far(list_ref, w3, w4, s2, s3, s4, given, far, sums, states):
    sums[...] = given[...]
    for at, ref in enumerate((s2, s3, s4)):
        states[(at + 2) * BLK : (at + 3) * BLK] = ref[...]
    for chunk, w_ref in ((3, w3), (4, w4)):
        add_spread(chunk, list_ref, w_ref, states, sums, list_ref[BEFORE + chunk], list_ref[TOTALS + chunk])
    put_coded(far, sums, 3 * BLK)


def spread_rest(near_ref, list_ref, w1, w3, w4, s2, s3, s4, given, own, back, fore, sums, states):
    sums[...] = given[...]
    for at, ref in enumerate((s2, s3, s4)):
        states[(at + 2) * BLK : (at + 3) * BLK] = ref[...]
    add_spread(1, near_ref, w1, states, sums, 0, near_ref[TOTALS + 1])
    for chunk, w_ref in ((3, w3), (4, w4)):
        add_spread(chunk, list_ref, w_ref, states, sums, 0, list_ref[BEFORE + chunk])
    own[...] = sums[:BLK]
    put_coded(back, sums, BLK)
    put_coded(fore, sums, 2 * BLK)


def spread(lists, weights, states):
    sums = ((SPARE + 1, CH, ROWS), F32)
    held = ((5 * BLK, CH, ROWS), BF16)
    part = ((BLK * CH + 16, ROWS), jnp.int16)
    w0, w1, w2, w3, w4_far, w4 = weights
    (near,) = build(spread_near, 3, [sums], [held], *lists, w0, w2, *states[:2])
    (far,) = build(spread_far, 4, [part], [sums, held], lists[1], w3, w4_far, *states[2:], near)
    near, _ = lax.optimization_barrier((near, far))
    return *build(
        spread_rest, 4, [((BLK, CH, ROWS), F32), part, part], [sums, held],
        *lists, w1, w3, w4, *states[2:], near,
    ), far


def wide_exchange(v):
    one = from_wide(v, 1)
    partner = swap_core(v)
    other = from_wide(v, -1)
    across = swap_core(one)
    return [v, partner, one, other, across]


def exchange_rows(back, fore, far):
    return across_x(far), along_x(back, -1), along_x(fore, 1)


def add_rows(own, parts):
    first = lax.optimization_barrier(own + uncoded(parts[0]))
    return first + uncoded(parts[1]) + uncoded(parts[2])


def local(embeddings, seeds, neighbours):
    code = functools.partial(coded, wide=lax.axis_index(WIDE), x=lax.axis_index("x"))
    seeds_t = jnp.swapaxes(seeds, 1, 2)
    after = lambda v, *done: lax.optimization_barrier((v, *done))[0]
    ids = split_ids(neighbours)
    two, full = prepare(embeddings, seeds_t, ids)
    one = third_turned(full, ids)
    back_two = along_x(two, 1)
    above = from_wide(full, 1)
    below = from_wide(full, -1)
    fore_one = along_x(one, -1)
    back_one = along_x(one, 1)
    back_two, fore_one, back_one, late_full, late_two = lax.optimization_barrier(
        (back_two, fore_one, back_one, full, two)
    )
    partner = swap_core(late_full)
    far_two = along_x(back_two, 1)
    fore_two = along_x(late_two, -1)
    far_one = along_x(after(fore_one, partner), -1)

    near = make_plan(
        (0, 1, 2), [code(neighbours), code(joined_ids(back_two)), code(joined_ids(fore_one))]
    )
    w0, sums, rows, *near_cols = build(
        build_0, 4, [weights_of(0), SUM_BUF, rows_of(9), *columns(2)], [],
        near, two, one, back_two, back_one, fore_one, full, partner,
    )
    beside = swap_core(after(above, sums))
    w1, sums, *wide_cols = build(
        build_1, 4, [weights_of(1), SUM_BUF, *columns(2)], [], near, rows, above, below, sums
    )
    lists = make_plan((3,), [code(joined_ids(after(far_two, sums)))], near)
    w2, w3, sums, rows = build(
        build_2, 4, [weights_of(2), weights_of(3), SUM_BUF, rows_of(12)], [],
        lists, rows, fore_two, far_two, far_one, *near_cols, *wide_cols, sums,
    )
    part = ((BLK * CH + 16, ROWS), jnp.int16)
    scratch = [SUM_BUF, ((BLK, CH, ROWS), BF16)]
    w4_far, far = build(build_far, 4, [weights_of(4), part], scratch, lists, rows, beside, sums)
    w4, own, back, fore = build(
        build_rest, 4, [weights_of(4), ((BLK, SUMS, ROWS), F32), part, part], scratch,
        lists, rows, beside, after(sums, far),
    )
    lists = [near, lists]
    weights = [w0, w1, w2, w3, w4_far, w4]

    parts = exchange_rows(back, fore, far)
    degree = jnp.sum(own[:, CH:], axis=1) + sum(uncoded_degrees(p) for p in parts)
    scale = (ALPHA / degree)[:, None, :]
    prior = (1.0 - ALPHA) * seeds_t
    scores = add_rows(own[:, :CH], parts) * scale + prior
    for _ in range(ITERS - 1):
        states = wide_exchange(scores.astype(BF16))
        own, *parts = spread(lists, weights, states)
        scores = add_rows(own, exchange_rows(*parts)) * scale + prior
    return jnp.swapaxes(scores, 1, 2)


def solution(mesh):
    fine = Mesh(mesh.devices.reshape(4, 4, 2, 4), ("z", "y", "c", "x"))
    everywhere = ("z", "y", "c", "x")
    return jax.shard_map(
        local,
        mesh=fine,
        in_specs=(P(everywhere, None, None), P(everywhere, None, None), P(everywhere, None)),
        out_specs=P(everywhere, None, None),
        check_vma=False,
    )
```
